32 devices in a mesh: batch: 8 (over y, x, core), seq: 4 (over z).
Axes of the slice: x: 2, y: 2, z: 4, core: 2. Of those that a mesh axis runs over, the one named last changes fastest.
Arguments:
- hidden_in: bfloat16 [32, 512, 768], P('batch', 'seq'), may hold values from -6 to 6
- lengths: int32 [32], P('batch'), may hold values from 64 to 512, as said below
- w_qkv: bfloat16 [768, 2304], replicated, may hold values from -0.21875 to 0.21875
- b_q: bfloat16 [768], replicated, may hold values from -3 to 3
- b_v: bfloat16 [768], replicated, may hold values from -3 to 3
- w_o: bfloat16 [768, 768], replicated, may hold values from -2.5 to 2.5
- b_o: bfloat16 [768], replicated, may hold values from -3 to 3
- gain_one: bfloat16 [768], replicated, may hold values from 0.25 to 1.75
- shift_one: bfloat16 [768], replicated, may hold values from -3 to 3
- w_in: bfloat16 [768, 3072], replicated, may hold values from -0.21875 to 0.21875
- b_in: bfloat16 [3072], replicated, may hold values from -3 to 3
- w_out: bfloat16 [3072, 768], replicated, may hold values from -0.109375 to 0.109375
- b_out: bfloat16 [768], replicated, may hold values from -3 to 3
- gain_two: bfloat16 [768], replicated, may hold values from 0.25 to 1.75
- shift_two: bfloat16 [768], replicated, may hold values from -3 to 3
- cot_hidden: bfloat16 [32, 512, 768], P('batch', 'seq'), may hold values from -6 to 6
- cot_pooled: bfloat16 [32, 768], P('batch'), may hold values from -24 to 24
Outputs:
- out_hidden: bfloat16 [32, 512, 768], P('batch', 'seq')
- pooled: float32 [32, 768], P('batch')
- grad_in: bfloat16 [32, 512, 768], P('batch', 'seq')
- grad_w_qkv: float32 [768, 2304], P('batch', 'seq')
- grad_b_q: float32 [768], replicated
- grad_b_v: float32 [768], replicated
- grad_w_o: float32 [768, 768], P('batch', 'seq')
- grad_b_o: float32 [768], replicated
- grad_gain_one: float32 [768], replicated
- grad_shift_one: float32 [768], replicated
- grad_w_in: float32 [768, 3072], P('batch', 'seq')
- grad_b_in: float32 [3072], replicated
- grad_w_out: float32 [3072, 768], P('batch', 'seq')
- grad_b_out: float32 [768], replicated
- grad_gain_two: float32 [768], replicated
- grad_shift_two: float32 [768], replicated
The draws below stay inside these ranges and needn't reach their ends.
Inputs may be any that keep to these rules, and one draw needn't show every extreme that they name: `lengths`: of the 4 passages of each index of batch, one is at full length 512.
All inputs are finite; a program needn't handle non-finite values.
Results may differ from the reference program's by a relative error of at most 0.019.
Values may be sent and summed in bfloat16 or wider, within the bound.
A program may use at most 128 MiB of HBM per device.

```python
import jax
import jax.numpy as jnp
from jax import lax

D = 768
H = 12
FF = 3072
SEQ_LEN = 512
SEQS_DEV = 4
SEQS = 32


def draw_lengths(key, part):
    key = jax.random.fold_in(key, 7)
    key_base, key_pick = jax.random.split(key)
    group_count = SEQS // SEQS_DEV
    base_len = jax.random.randint(key_base, (group_count, SEQS_DEV), SEQ_LEN // 8, SEQ_LEN + 1)
    chosen = jax.random.randint(key_pick, (group_count, 1), 0, SEQS_DEV)
    is_full = jnp.arange(SEQS_DEV)[None, :] == chosen
    return jnp.where(is_full, SEQ_LEN, base_len).reshape(SEQS).astype(jnp.int32)


def with_spikes(entries, own_key, source, target, shards_of, factor):
    def block_of(axis_at):
        return (jnp.arange(entries.shape[axis_at]) // (entries.shape[axis_at] // shards_of)).reshape((-1,) + (1,) * (entries.ndim - 1 - axis_at))

    near = jax.random.permutation(own_key, shards_of)[block_of(target)]
    far = (block_of(target) + shards_of // 2) % shards_of
    return jnp.where((block_of(source) == near) | (block_of(source) == far), factor * entries, entries)


def steps_of(key, shape, cuts, least, largest):
    def one(axis_at, blocks):
        steps = jax.random.uniform(jax.random.fold_in(jax.random.fold_in(key, 6), axis_at), (blocks,), jnp.float32, least / len(cuts), largest / len(cuts))
        return jnp.repeat(jnp.exp(steps), shape[axis_at] // blocks).reshape((-1,) + (1,) * (len(shape) - axis_at - 1))

    loudness = one(*cuts[0])
    for cut in cuts[1:]:
        loudness = loudness * one(*cut)
    return loudness


def scatter_about(own_key, extent, deviation, bound, cuts=(), held_as=jnp.bfloat16):
    result = jax.random.normal(own_key, extent, jnp.float32) * deviation
    if len(cuts) > 0:
        result = steps_of(own_key, extent, cuts, -0.22, 0.18) * result
    return jnp.clip(result, min=-bound, max=bound).astype(held_as)


def noise_with(rng, dims, spread, reach, cuts, heavy, held_as=jnp.bfloat16):
    result = spread * jax.random.normal(rng, dims, jnp.float32)
    if cuts:
        result = result * steps_of(rng, dims, cuts, -0.22, 0.18)
    return jnp.clip(with_spikes(result, jax.random.fold_in(rng, 3), *heavy), -reach, reach).astype(held_as)


def setup_inputs(seed: int = 0) -> dict:
    seeds = jax.random.split(jax.random.key(seed), 18)
    return {
        "hidden_in": noise_with(seeds[0], (SEQS, SEQ_LEN, D), 1.0, 6.0, ((0, 8), (1, 4)), (0, 2, 8, 2.0)),
        "lengths": draw_lengths(jax.random.fold_in(seeds[17], 71), 0),
        "w_qkv": scatter_about(seeds[2], (D, 3 * D), D ** -0.5, 0.21875),
        "b_q": scatter_about(seeds[3], (D,), 0.5, 3.0),
        "b_v": scatter_about(seeds[4], (D,), 0.5, 3.0),
        "w_o": scatter_about(seeds[5], (D, D), (D * 4 // SEQ_LEN) ** -0.5, 2.5),
        "b_o": scatter_about(seeds[6], (D,), 0.5, 3.0),
        "gain_one": jnp.clip(1.0 + 0.15 * jax.random.normal(seeds[7], (D,), jnp.float32), 0.25, 1.75).astype(jnp.bfloat16),
        "shift_one": scatter_about(seeds[8], (D,), 0.5, 3.0),
        "w_in": scatter_about(seeds[9], (D, FF), D ** -0.5, 0.21875),
        "b_in": scatter_about(seeds[10], (FF,), 0.5, 3.0),
        "w_out": scatter_about(seeds[11], (FF, D), FF ** -0.5, 0.109375),
        "b_out": scatter_about(seeds[12], (D,), 0.5, 3.0),
        "gain_two": jnp.clip(1.0 + 0.15 * jax.random.normal(seeds[13], (D,), jnp.float32), 0.25, 1.75).astype(jnp.bfloat16),
        "shift_two": scatter_about(seeds[14], (D,), 0.5, 3.0),
        "cot_hidden": scatter_about(seeds[15], (SEQS, SEQ_LEN, D), 1.0, 6.0, ((0, 8), (1, 4))),
        "cot_pooled": scatter_about(seeds[16], (SEQS, D), 4.0, 24.0, ((0, 8),)),
    }


precise = lax.Precision.HIGHEST

@jax.custom_vjp
def low(v):
    return lax.optimization_barrier(v.astype(jnp.bfloat16)).astype(jnp.float32)

@jax.custom_vjp
def low_back(v):
    return v

def low_keep(v):
    return (low(v), None)

def low_pass(kept, grad):
    return (grad,)

def back_keep(v):
    return (v, None)

def back_low(kept, grad):
    return (low(grad),)
low.defvjp(low_keep, low_pass)
low_back.defvjp(back_keep, back_low)

def norm_rows(values, gain_vec, shift_vec):
    centre_val = lax.optimization_barrier(jnp.mean(values, -1, keepdims=True))
    centred = values - centre_val
    inv_std = lax.rsqrt(lax.optimization_barrier(jnp.mean(centred * centred, -1, keepdims=True)) + 1e-12)
    return centred * inv_std * gain_vec + shift_vec

def forward(inputs, params, seq_lengths):
    w_qkv, b_q, b_v, w_o, b_o, gain_one, shift_one, w_in, b_in, w_out, b_out, gain_two, shift_two = params
    group_size, seq_len, model_width = inputs.shape
    head_size = model_width // H
    flat_rows = inputs.reshape(group_size * seq_len, model_width)
    bias_all = jnp.concatenate([b_q, jnp.zeros_like(b_q), b_v])
    projected = jnp.dot(flat_rows, w_qkv, precision=precise) + bias_all
    queries = low(low_back(projected[:, :model_width])).reshape(group_size, seq_len, H, head_size)
    keys_all = low(low_back(projected[:, model_width:2 * model_width])).reshape(group_size, seq_len, H, head_size)
    values_all = low(low_back(projected[:, 2 * model_width:])).reshape(group_size, seq_len, H, head_size)
    scores = low_back(jnp.einsum('gqhd,gkhd->ghqk', queries, keys_all, precision=precise) * head_size ** (-0.5))
    key_live = jnp.arange(seq_len, dtype=jnp.int32)[None, :] < seq_lengths[:, None]
    scores = jnp.where(key_live[:, None, None, :], scores, -1e+30)
    row_max = lax.optimization_barrier(jnp.max(scores, -1, keepdims=True))
    expo_vals = jnp.exp(scores - row_max)
    probs_low = low(expo_vals / lax.optimization_barrier(jnp.sum(expo_vals, -1, keepdims=True)))
    mixed = jnp.einsum('ghqk,gkhd->gqhd', probs_low, values_all, precision=precise)
    attended = low(low_back(mixed.reshape(group_size * seq_len, model_width)))
    branch = low_back(jnp.dot(attended, w_o, precision=precise) + b_o)
    middle = norm_rows(flat_rows + branch, gain_one, shift_one)
    pre_act = low_back(jnp.dot(low(middle), w_in, precision=precise) + b_in)
    act_low = low(low_back(jax.nn.gelu(pre_act, approximate=False)))
    ffn_out = low_back(jnp.dot(act_low, w_out, precision=precise) + b_out)
    output_rows = norm_rows(middle + ffn_out, gain_two, shift_two).reshape(group_size, seq_len, model_width)
    live_rows = key_live.astype(jnp.float32)[:, :, None]
    pooled = lax.optimization_barrier(jnp.sum(output_rows * live_rows, 1)) / seq_lengths[:, None].astype(jnp.float32)
    return (output_rows, pooled)

def reference(hidden_in, lengths, w_qkv, b_q, b_v, w_o, b_o, gain_one, shift_one, w_in, b_in, w_out, b_out, gain_two, shift_two, cot_hidden, cot_pooled):
    params = tuple((weight.astype(jnp.float32) for weight in (w_qkv, b_q, b_v, w_o, b_o, gain_one, shift_one, w_in, b_in, w_out, b_out, gain_two, shift_two)))
    group_count = SEQS // SEQS_DEV

    def scan_step(totals, slices):
        inputs, seq_lengths, cot_rows, cot_pool = slices

        def wrapped(values_in, *weights):
            return forward(values_in, weights, seq_lengths)
        outputs, pullback = jax.vjp(wrapped, inputs.astype(jnp.float32), *params)
        gradients = pullback((cot_rows.astype(jnp.float32), cot_pool.astype(jnp.float32)))
        totals = tuple((running + update for running, update in zip(totals, gradients[1:])))
        return (totals, (outputs[0].astype(jnp.bfloat16), outputs[1], gradients[0].astype(jnp.bfloat16)))
    start_totals = tuple((jnp.zeros_like(weight) for weight in params))
    totals, (out_rows, pooled, grad_rows) = lax.scan(scan_step, start_totals, (hidden_in.reshape(group_count, SEQS_DEV, SEQ_LEN, D), lengths.reshape(group_count, SEQS_DEV), cot_hidden.reshape(group_count, SEQS_DEV, SEQ_LEN, D), cot_pooled.reshape(group_count, SEQS_DEV, D)))
    return (out_rows.reshape(SEQS, SEQ_LEN, D), pooled.reshape(SEQS, D), grad_rows.reshape(SEQS, SEQ_LEN, D), totals[0], totals[1], totals[2], totals[3], totals[4], totals[5], totals[6], totals[7], totals[8], totals[9], totals[10], totals[11], totals[12])
```

```python
import functools

import jax
import jax.numpy as jnp
from jax import lax
from jax.experimental import pallas as pl
from jax.experimental.pallas import tpu as pltpu
from jax.sharding import PartitionSpec as P

H = 12
BF = jnp.bfloat16
F32 = jnp.float32
MESH = pl.DeviceIdType.MESH
V_BQ, V_BV, V_BO, V_G1, V_S1, V_BOUT, V_G2, V_S2, V_CP, V_BIN = range(10)


def nn(a, b):
    return lax.dot_general(a, b, (((1,), (0,)), ((), ())), preferred_element_type=F32)


def nt(a, b):
    return lax.dot_general(a, b, (((1,), (1,)), ((), ())), preferred_element_type=F32)


def tn(a, b):
    return lax.dot_general(a, b, (((0,), (0,)), ((), ())), preferred_element_type=F32)


def aligned(index, size):
    return pl.ds(pl.multiple_of(index * size, size), size)


def norm_back(grad, normed, inv_std):
    first = jnp.mean(grad, 0, keepdims=True)
    second = jnp.mean(grad * normed, 0, keepdims=True)
    return inv_std * (grad - first - normed * second)


def layer_kernel(dims, *refs):
    seq_count, block_len, width, ff = dims
    (
        hidden_ref,
        cot_ref,
        len_ref,
        vec_ref,
        w_qkv_hbm,
        w_o_hbm,
        w_in_hbm,
        w_out_hbm,
        out_ref,
        gin_ref,
        pooled_ref,
        vecs_ref,
        gq_ref,
        go_ref,
        gi_ref,
        gt_ref,
        w_qkv,
        w_o,
        w_in,
        w_out,
        x_rows,
        cot_rows,
        x_t,
        qkv_t,
        expo,
        inv_sum,
        att_t,
        normed_one,
        middle_low,
        act,
        slope,
        normed_two,
        grad_second,
        grad_first,
        low_a,
        grad_att,
        grad_proj,
        rows_out,
        rows_gin,
        stage,
        vec_t,
        vec_cols,
        w_sem,
        out_sem,
        x_send,
        x_recv,
        c_send,
        c_recv,
        o_send,
        o_recv,
        g_send,
        g_recv,
        own_sem,
    ) = refs
    seq_len = seq_count * block_len
    head = width // H
    me_b = lax.axis_index("batch")
    me_s = lax.axis_index("seq")

    loads = []
    for k, (src, dst) in enumerate(
        ((w_qkv_hbm, w_qkv), (w_o_hbm, w_o), (w_in_hbm, w_in), (w_out_hbm, w_out))
    ):
        load = pltpu.make_async_copy(src, dst, w_sem.at[k])
        load.start()
        loads.append(load)

    barrier = pltpu.get_barrier_semaphore()
    for d in range(1, seq_count):
        pl.semaphore_signal(
            barrier,
            inc=1,
            device_id=(me_b, lax.rem(me_s + d, seq_count)),
            device_id_type=MESH,
        )
    pl.semaphore_wait(barrier, seq_count - 1)

    def exchange(src, dst, own, send_sem, recv_sem):
        copies = []
        for d in range(1, seq_count):
            to = lax.rem(me_s + d, seq_count)
            copy = pltpu.make_async_remote_copy(
                src_ref=src.at[to],
                dst_ref=dst.at[me_s],
                send_sem=send_sem.at[d],
                recv_sem=recv_sem.at[d],
                device_id=(me_b, to),
                device_id_type=MESH,
            )
            copy.start()
            copies.append(copy)
        copy = pltpu.make_async_copy(src.at[me_s], dst.at[me_s], own_sem.at[own])
        copy.start()
        copies.append(copy)
        return copies

    def finish(copies):
        for copy in copies:
            copy.wait()

    hidden_copies = exchange(hidden_ref, x_rows, 0, x_send, x_recv)

    vec_cols[...] = jnp.zeros((width, 128), F32)
    vec_t[...] = jnp.transpose(vec_ref[...].astype(F32))

    def column(index):
        return vec_t[:, index : index + 1]

    length = len_ref[0]
    inv_len = 1.0 / jnp.full((1, seq_len), length, jnp.int32).astype(F32)
    token_at = lax.broadcasted_iota(jnp.int32, (1, seq_len), 1)
    live = jnp.where(token_at < length, 1.0, 0.0).astype(F32)
    key_at = lax.broadcasted_iota(jnp.int32, (seq_len, 1), 0)
    key_bias = jnp.where(key_at < length, 0.0, -1e30).astype(F32)

    finish(hidden_copies)
    cot_copies = exchange(cot_ref, cot_rows, 1, c_send, c_recv)
    x_t[...] = jnp.transpose(x_rows[...].reshape(seq_len, width))

    loads[0].wait()
    scale = head ** (-0.5)
    qkv_t[0:width, :] = (
        (tn(w_qkv[:, 0:width], x_t[...]) + column(V_BQ)) * scale
    ).astype(BF)
    qkv_t[width : 2 * width, :] = tn(w_qkv[:, width : 2 * width], x_t[...]).astype(BF)
    qkv_t[2 * width :, :] = (tn(w_qkv[:, 2 * width :], x_t[...]) + column(V_BV)).astype(BF)

    def head_rows(h, third):
        return pl.ds(pl.multiple_of(h * head + third * width, head), head)

    def attend(h, carry):
        scores = tn(qkv_t[head_rows(h, 1), :], qkv_t[head_rows(h, 0), :]) + key_bias
        top = jnp.max(scores, 0, keepdims=True)
        weights = jnp.exp(scores - top)
        inverse = 1.0 / jnp.sum(weights, 0, keepdims=True)
        weights_low = weights.astype(BF)
        expo[aligned(h, seq_len), :] = weights_low
        inv_sum[aligned(h, 8), :] = jnp.broadcast_to(inverse, (8, seq_len))
        att_t[head_rows(h, 0), :] = (nn(qkv_t[head_rows(h, 2), :], weights_low) * inverse).astype(BF)
        return carry

    lax.fori_loop(0, H, attend, 0)

    loads[1].wait()
    summed = x_t[...].astype(F32) + (tn(w_o[...], att_t[...]) + column(V_BO))
    centred = summed - jnp.mean(summed, 0, keepdims=True)
    inv_one = lax.rsqrt(jnp.mean(centred * centred, 0, keepdims=True) + 1e-12)
    normed_one[...] = centred * inv_one
    middle_low[...] = (normed_one[...] * column(V_G1) + column(V_S1)).astype(BF)

    loads[2].wait()
    parts = ff // width
    for i in range(parts):
        rows = slice(i * width, (i + 1) * width)
        pre = tn(w_in[:, rows], middle_low[...]) + column(V_BIN + i)
        cumulative = 0.5 * (1.0 + lax.erf(pre * 0.7071067811865476))
        density = jnp.exp(-0.5 * pre * pre) * 0.3989422804014327
        act[rows, :] = (pre * cumulative).astype(BF)
        slope[rows, :] = (cumulative + pre * density).astype(BF)
    loads[3].wait()
    middle = normed_one[...] * column(V_G1) + column(V_S1)
    summed = middle + (tn(w_out[...], act[...]) + column(V_BOUT))
    centred = summed - jnp.mean(summed, 0, keepdims=True)
    inv_two = lax.rsqrt(jnp.mean(centred * centred, 0, keepdims=True) + 1e-12)
    normed_two[...] = centred * inv_two
    output = normed_two[...] * column(V_G2) + column(V_S2)
    pooled_col = jnp.sum(output * (live * inv_len), 1, keepdims=True)
    rows_out[...] = jnp.transpose(output.astype(BF)).reshape(seq_count, block_len, width)
    out_copies = exchange(rows_out, out_ref, 2, o_send, o_recv)

    finish(cot_copies)
    grad_final = jnp.transpose(cot_rows[...].reshape(seq_len, width)).astype(F32)
    grad_final = grad_final + column(V_CP) * (live * inv_len)
    vec_cols[:, 0:1] = jnp.sum(grad_final * normed_two[...], 1, keepdims=True)
    vec_cols[:, 1:2] = jnp.sum(grad_final, 1, keepdims=True)
    grad_second[...] = norm_back(grad_final * column(V_G2), normed_two[...], inv_two)
    low_a[...] = grad_second[...].astype(BF)
    vec_cols[:, 2:3] = jnp.sum(low_a[...].astype(F32), 1, keepdims=True)

    def put(value, dst, sem):
        rows, columns = value.shape
        stage[0:rows, 0:columns] = value.astype(BF)
        copy = pltpu.make_async_copy(stage.at[0:rows, 0:columns], dst, out_sem.at[sem])
        copy.start()
        copy.wait()

    for i in range(parts):
        rows = slice(i * width, (i + 1) * width)
        put(nt(act[rows, :], low_a[...]), gt_ref.at[rows, :], 0)

    for i in range(parts):
        rows = slice(i * width, (i + 1) * width)
        grad_act = nn(w_out[rows, :], low_a[...]).astype(BF)
        grad_pre = (grad_act.astype(F32) * slope[rows, :].astype(F32)).astype(BF)
        slope[rows, :] = grad_pre
        vec_cols[:, 3 + i : 4 + i] = jnp.sum(grad_pre.astype(F32), 1, keepdims=True)
    put(nt(middle_low[...], slope[...]), gi_ref, 0)
    grad_middle = grad_second[...] + nn(w_in[...], slope[...])

    vec_cols[:, 7:8] = jnp.sum(grad_middle * normed_one[...], 1, keepdims=True)
    vec_cols[:, 8:9] = jnp.sum(grad_middle, 1, keepdims=True)
    grad_first[...] = norm_back(grad_middle * column(V_G1), normed_one[...], inv_one)
    low_a[...] = grad_first[...].astype(BF)
    vec_cols[:, 9:10] = jnp.sum(low_a[...].astype(F32), 1, keepdims=True)
    put(nt(att_t[...], low_a[...]), go_ref, 0)
    grad_heads = nn(w_o[...], low_a[...])
    for h in range(H):
        rows = slice(h * head, (h + 1) * head)
        grad_att[rows, :] = (grad_heads[rows, :] * inv_sum[h * 8 : h * 8 + 1, :]).astype(BF)

    def attend_back(h, carry):
        grad = grad_att[head_rows(h, 0), :]
        inner = jnp.sum(grad.astype(F32) * att_t[head_rows(h, 0), :].astype(F32), 0, keepdims=True)
        weights_low = expo[aligned(h, seq_len), :]
        grad_probs = tn(qkv_t[head_rows(h, 2), :], grad)
        grad_scores = (weights_low.astype(F32) * (grad_probs - inner)).astype(BF)
        grad_proj[head_rows(h, 0), :] = (nn(qkv_t[head_rows(h, 1), :], grad_scores) * scale).astype(BF)
        grad_proj[head_rows(h, 1), :] = nt(qkv_t[head_rows(h, 0), :], grad_scores).astype(BF)
        grad_proj[head_rows(h, 2), :] = nt(grad, weights_low).astype(BF)
        return carry

    lax.fori_loop(0, H, attend_back, 0)
    vec_cols[:, 10:11] = jnp.sum(grad_proj[0:width, :].astype(F32), 1, keepdims=True)
    vec_cols[:, 11:12] = jnp.sum(grad_proj[2 * width :, :].astype(F32), 1, keepdims=True)
    vec_cols[:, 12:13] = pooled_col
    grad_in = nn(w_qkv[...], grad_proj[...]) + grad_first[...]
    rows_gin[...] = jnp.transpose(grad_in.astype(BF)).reshape(seq_count, block_len, width)
    gin_copies = exchange(rows_gin, gin_ref, 3, g_send, g_recv)
    put(nt(x_t[...], grad_proj[...]), gq_ref, 0)
    vecs_ref[...] = jnp.transpose(vec_cols[...])[0:16, :]
    pooled_ref[...] = jnp.transpose(vec_cols[...])[8:16, :]
    finish(out_copies)
    finish(gin_copies)


def body(
    hidden_in,
    lengths,
    w_qkv,
    b_q,
    b_v,
    w_o,
    b_o,
    gain_one,
    shift_one,
    w_in,
    b_in,
    w_out,
    b_out,
    gain_two,
    shift_two,
    cot_hidden,
    cot_pooled,
):
    seq_count = lax.axis_size("seq")
    seqs_here, block_len, width = hidden_in.shape
    ff = w_in.shape[1]
    seq_len = seq_count * block_len
    assert seqs_here == seq_count
    me_s = lax.axis_index("seq")
    own_length = lax.dynamic_slice(lengths, (me_s,), (1,))
    own_cot = lax.dynamic_slice(cot_pooled, (me_s, 0), (1, width)).reshape(width)
    vectors = (b_q, b_v, b_o, gain_one, shift_one, b_out, gain_two, shift_two, own_cot, b_in)
    vec = jnp.concatenate(vectors).reshape(-1, width)
    vec = jnp.pad(vec, ((0, 128 - vec.shape[0]), (0, 0)))

    anywhere = pl.BlockSpec(memory_space=pl.ANY)
    vmem = pl.BlockSpec(memory_space=pltpu.VMEM)
    smem = pl.BlockSpec(memory_space=pltpu.SMEM)
    rows = jax.ShapeDtypeStruct(hidden_in.shape, BF)
    outs = pl.pallas_call(
        functools.partial(layer_kernel, (seq_count, block_len, width, ff)),
        out_shape=(
            rows,
            rows,
            jax.ShapeDtypeStruct((8, width), F32),
            jax.ShapeDtypeStruct((16, width), F32),
            jax.ShapeDtypeStruct(w_qkv.shape, BF),
            jax.ShapeDtypeStruct(w_o.shape, BF),
            jax.ShapeDtypeStruct(w_in.shape, BF),
            jax.ShapeDtypeStruct(w_out.shape, BF),
        ),
        in_specs=[anywhere, anywhere, smem, vmem, anywhere, anywhere, anywhere, anywhere],
        out_specs=(anywhere, anywhere, vmem, vmem, anywhere, anywhere, anywhere, anywhere),
        scratch_shapes=[
            pltpu.VMEM(w_qkv.shape, BF),
            pltpu.VMEM(w_o.shape, BF),
            pltpu.VMEM(w_in.shape, BF),
            pltpu.VMEM(w_out.shape, BF),
            pltpu.VMEM((seq_count, block_len, width), BF),
            pltpu.VMEM((seq_count, block_len, width), BF),
            pltpu.VMEM((width, seq_len), BF),
            pltpu.VMEM((3 * width, seq_len), BF),
            pltpu.VMEM((H * seq_len, seq_len), BF),
            pltpu.VMEM((H * 8, seq_len), F32),
            pltpu.VMEM((width, seq_len), BF),
            pltpu.VMEM((width, seq_len), F32),
            pltpu.VMEM((width, seq_len), BF),
            pltpu.VMEM((ff, seq_len), BF),
            pltpu.VMEM((ff, seq_len), BF),
            pltpu.VMEM((width, seq_len), F32),
            pltpu.VMEM((width, seq_len), F32),
            pltpu.VMEM((width, seq_len), F32),
            pltpu.VMEM((width, seq_len), BF),
            pltpu.VMEM((width, seq_len), BF),
            pltpu.VMEM((3 * width, seq_len), BF),
            pltpu.VMEM((seq_count, block_len, width), BF),
            pltpu.VMEM((seq_count, block_len, width), BF),
            pltpu.VMEM((width, ff), BF),
            pltpu.VMEM((width, 128), F32),
            pltpu.VMEM((width, 128), F32),
            pltpu.SemaphoreType.DMA((4,)),
            pltpu.SemaphoreType.DMA((1,)),
        ]
        + [pltpu.SemaphoreType.DMA((seq_count,))] * 8
        + [pltpu.SemaphoreType.DMA((4,))],
        compiler_params=pltpu.CompilerParams(
            collective_id=0, has_side_effects=True, vmem_limit_bytes=60 * 2**20
        ),
        name="encoder_layer",
    )(hidden_in, cot_hidden, own_length, vec, w_qkv, w_o, w_in, w_out)
    out_hidden, grad_in, pooled_row, vecs, g_qkv, g_o, g_in, g_out = outs
    pooled = lax.all_gather(pooled_row[4], "seq", axis=0)

    def scatter(grad):
        part = lax.psum_scatter(grad.astype(F32), "batch", scatter_dimension=0, tiled=True)
        return lax.psum_scatter(
            part.astype(BF), "seq", scatter_dimension=1, tiled=True
        ).astype(F32)

    total = lax.psum(vecs[:12], ("batch", "seq"))
    return (
        out_hidden,
        pooled,
        grad_in,
        scatter(g_qkv),
        total[10],
        total[11],
        scatter(g_o),
        total[9],
        total[7],
        total[8],
        scatter(g_in),
        total[3:7].reshape(ff),
        scatter(g_out),
        total[2],
        total[0],
        total[1],
    )


def solution(mesh):
    rows = P("batch", "seq", None)
    shard = P("batch", "seq")
    in_specs = (rows, P("batch")) + (P(),) * 13 + (rows, P("batch", None))
    out_specs = (
        rows,
        P("batch", None),
        rows,
        shard,
        P(),
        P(),
        shard,
        P(),
        P(),
        P(),
        shard,
        P(),
        shard,
        P(),
        P(),
        P(),
    )
    return jax.shard_map(body, mesh=mesh, in_specs=in_specs, out_specs=out_specs, check_vma=False)
```

```python
import functools

import jax
import jax.numpy as jnp
from jax import lax
from jax.experimental import pallas as pl
from jax.experimental.pallas import tpu as pltpu
from jax.sharding import PartitionSpec as P

H = 12
BF = jnp.bfloat16
F32 = jnp.float32
MESH = pl.DeviceIdType.MESH
V_BQ, V_BV, V_BO, V_G1, V_S1, V_BOUT, V_G2, V_S2, V_CP, V_BIN = range(10)


def nn(a, b):
    return lax.dot_general(a, b, (((1,), (0,)), ((), ())), preferred_element_type=F32)


def nt(a, b):
    return lax.dot_general(a, b, (((1,), (1,)), ((), ())), preferred_element_type=F32)


def tn(a, b):
    return lax.dot_general(a, b, (((0,), (0,)), ((), ())), preferred_element_type=F32)


def aligned(index, size):
    return pl.ds(pl.multiple_of(index * size, size), size)


def norm_back(grad, normed, inv_std):
    first = jnp.mean(grad, 0, keepdims=True)
    second = jnp.mean(grad * normed, 0, keepdims=True)
    return inv_std * (grad - first - normed * second)


def add_low(a, b):
    return (a.astype(F32) + b.astype(F32)).astype(BF)


G_OUT, G_IN, G_O, G_QKV = range(4)


def layer_kernel(dims, *refs):
    batch_count, seq_count, block_len, width, ff, fused = dims
    refs = list(refs)

    def take(count):
        taken = refs[:count]
        del refs[:count]
        return taken

    hidden_ref, cot_ref, len_ref, cot_pool_ref = take(4)
    vectors = take(9)
    w_qkv_hbm, w_o_hbm, w_in_hbm, w_out_hbm = take(4)
    out_ref, gin_ref, pooled_ref, vecs_ref = take(4)
    grad_refs = take(4)
    w_qkv, w_o, w_in, w_out = take(4)
    x_rows, cot_rows, x_t, qkv_t, expo, inv_sum, att_t = take(7)
    normed_one, middle_low, act, slope, normed_two, grad_second, low_a, grad_att = take(8)
    vec_cols, w_sem, own_sem = take(3)
    x_send, x_recv, c_send, c_recv, o_send, o_recv, g_send, g_recv = take(8)
    if fused:
        send_core = take(3)
        held_core, held_one, held_two, held_z, z_one, z_two = (take(4) for _ in range(6))
        core_send, core_recv, link_send, link_recv = take(4)
        vec_own, vec_in, pool_own, pool_in, v_send, v_recv, p_send, p_recv = take(8)
    else:
        stage, put_sem = take(2)
    seq_len = seq_count * block_len
    head = width // H
    parts = ff // width
    me_b = lax.axis_index("batch")
    me_s = lax.axis_index("seq")

    loads = []
    for k, (src, dst) in enumerate(
        ((w_qkv_hbm, w_qkv), (w_o_hbm, w_o), (w_in_hbm, w_in), (w_out_hbm, w_out))
    ):
        load = pltpu.make_async_copy(src, dst, w_sem.at[k])
        load.start()
        loads.append(load)

    def flipped(index, bit):
        return index + bit - 2 * bit * lax.rem(index // bit, 2)

    def seq_peer(d):
        return (me_b, lax.rem(me_s + d, seq_count))

    core, at_x, at_y = lax.rem(me_b, 2), lax.rem(me_b // 2, 2), lax.rem(me_b // 4, 2)
    z_lo, z_hi = lax.rem(me_s, 2), lax.rem(me_s // 2, 2)
    to_core, to_x, to_y = ((flipped(me_b, bit), me_s) for bit in (1, 2, 4))
    to_z_lo, to_z_hi = ((me_b, flipped(me_s, bit)) for bit in (1, 2))

    barrier = pltpu.get_barrier_semaphore()
    greeted = [seq_peer(d) for d in range(1, seq_count)]
    if fused:
        greeted += [to_core, to_x, to_y]
    for device in greeted:
        pl.semaphore_signal(barrier, inc=1, device_id=device, device_id_type=MESH)
    pl.semaphore_wait(barrier, len(greeted))

    def remote(src, dst, device, send_sem, recv_sem):
        copy = pltpu.make_async_remote_copy(
            src_ref=src,
            dst_ref=dst,
            send_sem=send_sem,
            recv_sem=recv_sem,
            device_id=device,
            device_id_type=MESH,
        )
        copy.start()
        return copy

    def exchange(src, dst, own, send_sem, recv_sem):
        copies = []
        for d in range(1, seq_count):
            to = lax.rem(me_s + d, seq_count)
            copies.append(
                remote(src.at[to], dst.at[me_s], seq_peer(d), send_sem.at[d], recv_sem.at[d])
            )
        copy = pltpu.make_async_copy(src.at[me_s], dst.at[me_s], own_sem.at[own])
        copy.start()
        copies.append(copy)
        return copies

    def finish(copies):
        for copy in copies:
            copy.wait()

    hidden_copies = exchange(hidden_ref, x_rows, 0, x_send, x_recv)

    cot_pool = cot_pool_ref[...].astype(F32)
    is_mine = lax.broadcasted_iota(jnp.int32, cot_pool.shape, 0) == me_s
    cot_pool = jnp.sum(jnp.where(is_mine, cot_pool, 0.0), 0, keepdims=True)
    rows = [ref[...].astype(F32).reshape(1, width) for ref in vectors[:8]] + [cot_pool]
    for i in range(parts):
        rows.append(vectors[8][i * width : (i + 1) * width].astype(F32).reshape(1, width))
    rows.append(jnp.zeros((128 - len(rows), width), F32))
    vec_t = jnp.transpose(jnp.concatenate(rows, 0))
    vec_cols[...] = jnp.zeros((width, 128), F32)

    def column(index):
        return vec_t[:, index : index + 1]

    length = len_ref[me_s]
    inv_len = 1.0 / jnp.full((1, seq_len), length, jnp.int32).astype(F32)
    token_at = lax.broadcasted_iota(jnp.int32, (1, seq_len), 1)
    live = jnp.where(token_at < length, 1.0, 0.0).astype(F32)
    key_at = lax.broadcasted_iota(jnp.int32, (seq_len, 1), 0)
    key_bias = jnp.where(key_at < length, 0.0, -1e30).astype(F32)

    finish(hidden_copies)
    cot_copies = exchange(cot_ref, cot_rows, 1, c_send, c_recv)
    x_t[...] = jnp.transpose(x_rows[...].reshape(seq_len, width))

    loads[0].wait()
    scale = head ** (-0.5)
    qkv_t[0:width, :] = (
        (tn(w_qkv[:, 0:width], x_t[...]) + column(V_BQ)) * scale
    ).astype(BF)
    qkv_t[width : 2 * width, :] = tn(w_qkv[:, width : 2 * width], x_t[...]).astype(BF)
    qkv_t[2 * width :, :] = (tn(w_qkv[:, 2 * width :], x_t[...]) + column(V_BV)).astype(BF)

    def head_rows(h, third):
        return pl.ds(pl.multiple_of(h * head + third * width, head), head)

    def attend(h, carry):
        scores = tn(qkv_t[head_rows(h, 1), :], qkv_t[head_rows(h, 0), :]) + key_bias
        top = jnp.max(scores, 0, keepdims=True)
        weights = jnp.exp(scores - top)
        inverse = 1.0 / jnp.sum(weights, 0, keepdims=True)
        weights_low = weights.astype(BF)
        expo[aligned(h, seq_len), :] = weights_low
        inv_sum[aligned(h, 8), :] = jnp.broadcast_to(inverse, (8, seq_len))
        att_t[head_rows(h, 0), :] = (nn(qkv_t[head_rows(h, 2), :], weights_low) * inverse).astype(BF)
        return carry

    lax.fori_loop(0, H, attend, 0)

    loads[1].wait()
    summed = x_t[...].astype(F32) + (tn(w_o[...], att_t[...]) + column(V_BO))
    centred = summed - jnp.mean(summed, 0, keepdims=True)
    inv_one = lax.rsqrt(jnp.mean(centred * centred, 0, keepdims=True) + 1e-12)
    normed_one[...] = centred * inv_one
    middle_low[...] = (normed_one[...] * column(V_G1) + column(V_S1)).astype(BF)

    loads[2].wait()
    for i in range(parts):
        rows = slice(i * width, (i + 1) * width)
        pre = tn(w_in[:, rows], middle_low[...]) + column(V_BIN + i)
        cumulative = 0.5 * (1.0 + lax.erf(pre * 0.7071067811865476))
        density = jnp.exp(-0.5 * pre * pre) * 0.3989422804014327
        act[rows, :] = (pre * cumulative).astype(BF)
        slope[rows, :] = (cumulative + pre * density).astype(BF)
    loads[3].wait()
    middle = normed_one[...] * column(V_G1) + column(V_S1)
    summed = middle + (tn(w_out[...], act[...]) + column(V_BOUT))
    centred = summed - jnp.mean(summed, 0, keepdims=True)
    inv_two = lax.rsqrt(jnp.mean(centred * centred, 0, keepdims=True) + 1e-12)
    normed_two[...] = centred * inv_two
    output = normed_two[...] * column(V_G2) + column(V_S2)
    pooled_col = jnp.sum(output * (live * inv_len), 1, keepdims=True)
    rows_out = x_rows
    rows_out[...] = jnp.transpose(output.astype(BF)).reshape(seq_count, block_len, width)
    out_copies = exchange(rows_out, out_ref, 2, o_send, o_recv)

    finish(cot_copies)
    grad_final = jnp.transpose(cot_rows[...].reshape(seq_len, width)).astype(F32)
    grad_final = grad_final + column(V_CP) * (live * inv_len)
    vec_cols[:, 0:1] = jnp.sum(grad_final * normed_two[...], 1, keepdims=True)
    vec_cols[:, 1:2] = jnp.sum(grad_final, 1, keepdims=True)
    grad_second[...] = norm_back(grad_final * column(V_G2), normed_two[...], inv_two)
    low_a[...] = grad_second[...].astype(BF)
    vec_cols[:, 2:3] = jnp.sum(low_a[...].astype(F32), 1, keepdims=True)

    def whole_grad(m):
        if m == G_OUT:
            rows, columns = act, low_a
        elif m == G_IN:
            rows, columns = middle_low, slope
        elif m == G_O:
            rows, columns = att_t, low_a
        else:
            rows, columns = x_t, qkv_t
        return rows, columns

    def put(m):
        rows, columns = whole_grad(m)
        for i in range(rows.shape[0] // width):
            value = nt(rows[i * width : (i + 1) * width, :], columns[...])
            here = stage.at[:, 0 : value.shape[1]]
            here[...] = value.astype(BF)
            copy = pltpu.make_async_copy(
                here, grad_refs[m].at[i * width : (i + 1) * width, :], put_sem.at[0]
            )
            copy.start()
            copy.wait()

    flight = {}

    def partial(m, which):
        rows, columns = whole_grad(m)
        deep = rows.shape[0] // batch_count
        picked = [rows[aligned(2 * j + which, deep), :] for j in range(4)]
        value = nt(jnp.concatenate(picked, 0), columns[...])
        half = value.shape[1] // 2
        tile = half // parts if m == G_IN else half
        for j in range(4):
            for h in range(2):
                for t in range(half // tile):
                    start = h * half + t * tile
                    block = value[j * deep : (j + 1) * deep, start : start + tile]
                    yield h, j, slice(t * deep, (t + 1) * deep), block

    def core_buffer(m):
        return send_core[max(m - 1, 0)]

    def to_core_start(m):
        buffer = core_buffer(m)
        if m == G_IN:
            for copy in flight[G_OUT, 0]:
                copy.wait_send()
        for h, j, rows, block in partial(m, 1 - core):
            buffer[h, j // 2, j % 2, rows, :] = block.astype(BF)
        flight[m, 0] = [
            remote(buffer, held_core[m], to_core, core_send.at[m, 0], core_recv.at[m, 0])
        ]

    def to_core_add(m):
        finish(flight[m, 0]) if m != G_OUT else None
        held = held_core[m]
        for h, j, rows, block in partial(m, core):
            held[h, j // 2, j % 2, rows, :] = add_low(held[h, j // 2, j % 2, rows, :], block)
        flight[m, 1] = [
            remote(
                held.at[0, :, 1 - at_x],
                held_one[m].at[0],
                to_x,
                link_send.at[m, 0],
                link_recv.at[m, 0],
            ),
            remote(
                held.at[1, 1 - at_y],
                held_one[m].at[1],
                to_y,
                link_send.at[m, 1],
                link_recv.at[m, 1],
            ),
        ]

    order = ((1 - at_y, 1 - at_x), (at_y, 1 - at_x), (1 - at_y, at_x), (at_y, at_x))

    def first_block(y, x, which):
        deep = ff // batch_count
        row = aligned(4 * y + 2 * x + which, deep)
        return nt(act[row, :], low_a[...])

    def first_start():
        buffer = send_core[0]
        copies = []
        for k, (y, x) in enumerate(order):
            value = first_block(y, x, 1 - core)
            half = value.shape[1] // 2
            buffer[0, y, x] = value[:, :half].astype(BF)
            buffer[1, y, x] = value[:, half:].astype(BF)
            copies.append(
                remote(
                    buffer.at[:, y, x],
                    held_core[G_OUT].at[:, y, x],
                    to_core,
                    core_send.at[G_OUT, k],
                    core_recv.at[G_OUT, k],
                )
            )
        flight[G_OUT, 0] = copies

    def first_add():
        held, after = held_core[G_OUT], held_one[G_OUT]
        copies = []
        for k, (y, x) in enumerate(order):
            flight[G_OUT, 0][k].wait_recv()
            value = first_block(y, x, core)
            half = value.shape[1] // 2
            held[0, y, x] = add_low(held[0, y, x], value[:, :half])
            held[1, y, x] = add_low(held[1, y, x], value[:, half:])
            if k in (0, 1):
                copies.append(
                    remote(
                        held.at[0, y, x],
                        after.at[0, y],
                        to_x,
                        link_send.at[G_OUT, k],
                        link_recv.at[G_OUT, k],
                    )
                )
            if k in (0, 2):
                copies.append(
                    remote(
                        held.at[1, y, x],
                        after.at[1, x],
                        to_y,
                        link_send.at[G_OUT, 2 + k // 2],
                        link_recv.at[G_OUT, 2 + k // 2],
                    )
                )
        flight[G_OUT, 1] = copies

    def second_link(m):
        finish(flight[m, 1])
        held, after = held_core[m], held_one[m]
        after[0, 1 - at_y] = add_low(after[0, 1 - at_y], held[0, 1 - at_y, at_x])
        after[1, 1 - at_x] = add_low(after[1, 1 - at_x], held[1, at_y, 1 - at_x])
        flight[m, 2] = [
            remote(
                after.at[0, 1 - at_y],
                held_two[m].at[0],
                to_y,
                link_send.at[m, 4],
                link_recv.at[m, 4],
            ),
            remote(
                after.at[1, 1 - at_x],
                held_two[m].at[1],
                to_x,
                link_send.at[m, 5],
                link_recv.at[m, 5],
            ),
        ]
        after[0, at_y] = add_low(after[0, at_y], held[0, at_y, at_x])
        after[1, at_x] = add_low(after[1, at_x], held[1, at_y, at_x])

    def first_z(m):
        finish(flight[m, 2])
        after, last, ready = held_one[m], held_two[m], held_z[m]
        for h in range(2):
            mine = after[0, at_y] if h == 0 else after[1, at_x]
            block = add_low(last[h], mine)
            deep, wide = block.shape
            for k in range(2):
                if m == G_IN:
                    ready[h, k] = block[k * (deep // 2) : (k + 1) * (deep // 2), :]
                else:
                    ready[h, k, :, : wide // 2] = block[:, k * (wide // 2) : (k + 1) * (wide // 2)]
        flight[m, 3] = [
            remote(
                ready.at[:, 1 - z_lo], z_one[m], to_z_lo, link_send.at[m, 6], link_recv.at[m, 6]
            )
        ]

    def second_z(m):
        finish(flight[m, 3])
        z_one[m][1 - z_hi] = add_low(z_one[m][1 - z_hi], held_z[m][1 - z_hi, z_lo])
        flight[m, 4] = [
            remote(
                z_one[m].at[1 - z_hi], z_two[m], to_z_hi, link_send.at[m, 7], link_recv.at[m, 7]
            )
        ]

    def last_sum(m):
        mine = z_one[m][z_hi].astype(F32) + held_z[m][z_hi, z_lo].astype(F32)
        finish(flight[m, 4])
        total = mine + z_two[m][...].astype(F32)
        out = grad_refs[m]
        deep, wide = out.shape
        if m == G_IN:
            out[:, : wide // 2] = total[:deep, :]
            out[:, wide // 2 :] = total[deep:, :]
        else:
            out[...] = total[:, :wide]

    peers = (to_core, to_x, to_y, to_z_lo, to_z_hi)

    def vector_start(g):
        vec_own[g, 0] = jnp.transpose(vec_cols[...])[8 * g : 8 * g + 8, :]
        flight["v", g] = remote(
            vec_own.at[g, 0], vec_in.at[g, 0], peers[0], v_send.at[g, 0], v_recv.at[g, 0]
        )

    def vector_step(g, k):
        flight["v", g].wait()
        total = vec_own[g, k] + vec_in[g, k]
        if k == 4:
            vecs_ref[8 * g : 8 * g + 8, :] = total
        else:
            vec_own[g, k + 1] = total
            flight["v", g] = remote(
                vec_own.at[g, k + 1],
                vec_in.at[g, k + 1],
                peers[k + 1],
                v_send.at[g, k + 1],
                v_recv.at[g, k + 1],
            )

    if fused:
        first_start()
        for m in (G_OUT, G_O, G_QKV):
            held_z[m][...] = jnp.zeros_like(held_z[m])
        pool_own[...] = jnp.transpose(jnp.broadcast_to(pooled_col, (width, 128)))[0:8, :]
        pool_in[me_s] = pool_own[...]
        flight["p"] = [
            remote(pool_own, pool_in.at[me_s], seq_peer(d), p_send.at[d], p_recv.at[d])
            for d in range(1, seq_count)
        ]
        first_add()
    else:
        vec_cols[:, 12:13] = pooled_col
        put(G_OUT)

    for i in range(parts):
        rows = slice(i * width, (i + 1) * width)
        grad_act_low = nn(w_out[rows, :], low_a[...]).astype(BF)
        grad_pre = (grad_act_low.astype(F32) * slope[rows, :].astype(F32)).astype(BF)
        slope[rows, :] = grad_pre
        vec_cols[:, 3 + i : 4 + i] = jnp.sum(grad_pre.astype(F32), 1, keepdims=True)
    if fused:
        to_core_start(G_IN)
    else:
        put(G_IN)
    grad_middle = grad_second[...] + nn(w_in[...], slope[...])

    vec_cols[:, 7:8] = jnp.sum(grad_middle * normed_one[...], 1, keepdims=True)
    vec_cols[:, 8:9] = jnp.sum(grad_middle, 1, keepdims=True)
    grad_first = normed_two
    grad_first[...] = norm_back(grad_middle * column(V_G1), normed_one[...], inv_one)
    low_a[...] = grad_first[...].astype(BF)
    vec_cols[:, 9:10] = jnp.sum(low_a[...].astype(F32), 1, keepdims=True)
    if fused:
        to_core_add(G_IN)
        to_core_start(G_O)
        vector_start(0)
    else:
        put(G_O)
    grad_heads = nn(w_o[...], low_a[...])
    for h in range(H):
        rows = slice(h * head, (h + 1) * head)
        grad_att[rows, :] = (grad_heads[rows, :] * inv_sum[h * 8 : h * 8 + 1, :]).astype(BF)
    if fused:
        second_link(G_OUT)
        to_core_add(G_O)
        vector_step(0, 0)

    def attend_back(h, carry):
        grad = grad_att[head_rows(h, 0), :]
        inner = jnp.sum(grad.astype(F32) * att_t[head_rows(h, 0), :].astype(F32), 0, keepdims=True)
        weights_low = expo[aligned(h, seq_len), :]
        queries, keys, values = (qkv_t[head_rows(h, third), :] for third in range(3))
        grad_probs = tn(values, grad)
        grad_scores = (weights_low.astype(F32) * (grad_probs - inner)).astype(BF)
        qkv_t[head_rows(h, 0), :] = (nn(keys, grad_scores) * scale).astype(BF)
        qkv_t[head_rows(h, 1), :] = nt(queries, grad_scores).astype(BF)
        qkv_t[head_rows(h, 2), :] = nt(grad, weights_low).astype(BF)
        return carry

    if fused:
        for k in range(3):
            lax.fori_loop(k * (H // 3), (k + 1) * (H // 3), attend_back, 0)
            vector_step(0, k + 1)
    else:
        lax.fori_loop(0, H, attend_back, 0)
    vec_cols[:, 10:11] = jnp.sum(qkv_t[0:width, :].astype(F32), 1, keepdims=True)
    vec_cols[:, 11:12] = jnp.sum(qkv_t[2 * width :, :].astype(F32), 1, keepdims=True)
    if fused:
        to_core_start(G_QKV)
        vector_start(1)
        vector_step(0, 4)
    grad_in = nn(w_qkv[...], qkv_t[...]) + grad_first[...]
    rows_gin = cot_rows
    rows_gin[...] = jnp.transpose(grad_in.astype(BF)).reshape(seq_count, block_len, width)
    gin_copies = exchange(rows_gin, gin_ref, 3, g_send, g_recv)
    if fused:
        to_core_add(G_QKV)
        vector_step(1, 0)
        second_link(G_IN)
        first_z(G_OUT)
        second_link(G_O)
        vector_step(1, 1)
        second_z(G_OUT)
        second_link(G_QKV)
        first_z(G_IN)
        last_sum(G_OUT)
        first_z(G_O)
        vector_step(1, 2)
        second_z(G_IN)
        second_z(G_O)
        last_sum(G_IN)
        first_z(G_QKV)
        last_sum(G_O)
        vector_step(1, 3)
        second_z(G_QKV)
        vector_step(1, 4)
        finish(flight["p"])
        for k in range(seq_count):
            pooled_ref[k : k + 1, :] = pool_in[k, 0:1, :]
        last_sum(G_QKV)
        for copy in flight[G_OUT, 0]:
            pass
    else:
        put(G_QKV)
        vecs_ref[...] = jnp.transpose(vec_cols[...])[0:16, :]
        pooled_ref[...] = jnp.transpose(vec_cols[...])[12:16, :]
    finish(out_copies)
    finish(gin_copies)


def body(
    hidden_in,
    lengths,
    w_qkv,
    b_q,
    b_v,
    w_o,
    b_o,
    gain_one,
    shift_one,
    w_in,
    b_in,
    w_out,
    b_out,
    gain_two,
    shift_two,
    cot_hidden,
    cot_pooled,
):
    batch_count, seq_count = lax.axis_size("batch"), lax.axis_size("seq")
    seqs_here, block_len, width = hidden_in.shape
    ff = w_in.shape[1]
    seq_len = seq_count * block_len
    assert seqs_here == seq_count
    fused = batch_count == 8 and seq_count == 4

    anywhere = pl.BlockSpec(memory_space=pl.ANY)
    vmem = pl.BlockSpec(memory_space=pltpu.VMEM)
    smem = pl.BlockSpec(memory_space=pltpu.SMEM)
    rows = jax.ShapeDtypeStruct(hidden_in.shape, BF)
    weights = (w_out, w_in, w_o, w_qkv)
    if fused:
        grads = tuple(
            jax.ShapeDtypeStruct((w.shape[0] // batch_count, w.shape[1] // seq_count), F32)
            for w in weights
        )
    else:
        grads = tuple(jax.ShapeDtypeStruct(w.shape, BF) for w in weights)
    dma = pltpu.SemaphoreType.DMA
    scratch = [pltpu.VMEM(w.shape, BF) for w in (w_qkv, w_o, w_in, w_out)]
    scratch += [
        pltpu.VMEM((seq_count, block_len, width), BF),
        pltpu.VMEM((seq_count, block_len, width), BF),
        pltpu.VMEM((width, seq_len), BF),
        pltpu.VMEM((3 * width, seq_len), BF),
        pltpu.VMEM((H * seq_len, seq_len), BF),
        pltpu.VMEM((H * 8, seq_len), F32),
        pltpu.VMEM((width, seq_len), BF),
        pltpu.VMEM((width, seq_len), F32),
        pltpu.VMEM((width, seq_len), BF),
        pltpu.VMEM((ff, seq_len), BF),
        pltpu.VMEM((ff, seq_len), BF),
        pltpu.VMEM((width, seq_len), F32),
        pltpu.VMEM((width, seq_len), F32),
        pltpu.VMEM((width, seq_len), BF),
        pltpu.VMEM((width, seq_len), BF),
        pltpu.VMEM((width, 128), F32),
        dma((4,)),
        dma((4,)),
    ]
    scratch += [dma((seq_count,))] * 8
    if fused:
        deep = width // batch_count
        blocks = (
            (ff // batch_count, width // 2),
            (deep * (ff // width), width // 2),
            (deep, width // 2),
            (deep, 3 * width // 2),
        )
        wide = [-(-w.shape[1] // seq_count // 128) * 128 for w in weights]
        z_blocks = (
            (ff // batch_count, wide[0]),
            (deep * (ff // width) // 2, width // 2),
            (deep, wide[2]),
            (deep, wide[3]),
        )
        scratch += [pltpu.VMEM((2, 2, 2) + blocks[m], BF) for m in (0, 2, 3)]
        scratch += [pltpu.VMEM((2, 2, 2) + block, BF) for block in blocks]
        scratch += [pltpu.VMEM((2, 2) + block, BF) for block in blocks]
        scratch += [pltpu.VMEM((2,) + block, BF) for block in blocks]
        scratch += [pltpu.VMEM((2, 2) + block, BF) for block in z_blocks]
        scratch += [pltpu.VMEM((2,) + block, BF) for block in z_blocks]
        scratch += [pltpu.VMEM(block, BF) for block in z_blocks]
        scratch += [dma((4, 4)), dma((4, 4)), dma((4, 8)), dma((4, 8))]
        scratch += [
            pltpu.VMEM((2, 5, 8, width), F32),
            pltpu.VMEM((2, 5, 8, width), F32),
            pltpu.VMEM((8, width), F32),
            pltpu.VMEM((seq_count, 8, width), F32),
            dma((2, 5)),
            dma((2, 5)),
            dma((seq_count,)),
            dma((seq_count,)),
        ]
    else:
        scratch += [pltpu.VMEM((width, ff), BF), dma((1,))]
    outs = pl.pallas_call(
        functools.partial(
            layer_kernel, (batch_count, seq_count, block_len, width, ff, fused)
        ),
        out_shape=(
            rows,
            rows,
            jax.ShapeDtypeStruct((seq_count, width), F32),
            jax.ShapeDtypeStruct((16, width), F32),
        )
        + grads,
        in_specs=[anywhere, anywhere, smem] + [vmem] * 10 + [anywhere] * 4,
        out_specs=(anywhere, anywhere, vmem, vmem) + (vmem if fused else anywhere,) * 4,
        scratch_shapes=scratch,
        compiler_params=pltpu.CompilerParams(
            collective_id=0, has_side_effects=True, vmem_limit_bytes=63 * 2**20
        ),
        name="encoder_layer",
    )(
        hidden_in,
        cot_hidden,
        lengths,
        cot_pooled,
        b_q,
        b_v,
        b_o,
        gain_one,
        shift_one,
        b_out,
        gain_two,
        shift_two,
        b_in,
        w_qkv,
        w_o,
        w_in,
        w_out,
    )
    out_hidden, grad_in, pooled, total, g_out, g_in, g_o, g_qkv = outs
    if not fused:
        pooled = lax.all_gather(pooled[0], "seq", axis=0)
        total = lax.psum(total[:12], ("batch", "seq"))

        def scatter(grad):
            part = lax.psum_scatter(grad.astype(F32), "batch", scatter_dimension=0, tiled=True)
            part = lax.psum_scatter(part.astype(BF), "seq", scatter_dimension=1, tiled=True)
            return part.astype(F32)

        g_out, g_in, g_o, g_qkv = (scatter(g) for g in (g_out, g_in, g_o, g_qkv))
    return (
        out_hidden,
        pooled,
        grad_in,
        g_qkv,
        total[10],
        total[11],
        g_o,
        total[9],
        total[7],
        total[8],
        g_in,
        total[3:7].reshape(ff),
        g_out,
        total[2],
        total[0],
        total[1],
    )


def solution(mesh):
    rows = P("batch", "seq", None)
    shard = P("batch", "seq")
    in_specs = (rows, P("batch")) + (P(),) * 13 + (rows, P("batch", None))
    out_specs = (
        rows,
        P("batch", None),
        rows,
        shard,
        P(),
        P(),
        shard,
        P(),
        P(),
        P(),
        shard,
        P(),
        shard,
        P(),
        P(),
        P(),
    )
    return jax.shard_map(body, mesh=mesh, in_specs=in_specs, out_specs=out_specs, check_vma=False)
```

```python
import functools

import jax
import jax.numpy as jnp
from jax import lax
from jax.experimental import pallas as pl
from jax.experimental.pallas import tpu as pltpu
from jax.sharding import PartitionSpec as P

H = 12
BF = jnp.bfloat16
F32 = jnp.float32
MESH = pl.DeviceIdType.MESH
V_BQ, V_BV, V_BO, V_G1, V_S1, V_BOUT, V_G2, V_S2, V_CP, V_BIN = range(10)


def nn(a, b):
    return lax.dot_general(a, b, (((1,), (0,)), ((), ())), preferred_element_type=F32)


def nt(a, b):
    return lax.dot_general(a, b, (((1,), (1,)), ((), ())), preferred_element_type=F32)


def tn(a, b):
    return lax.dot_general(a, b, (((0,), (0,)), ((), ())), preferred_element_type=F32)


def aligned(index, size):
    return pl.ds(pl.multiple_of(index * size, size), size)


def norm_back(grad, normed, inv_std):
    first = jnp.mean(grad, 0, keepdims=True)
    second = jnp.mean(grad * normed, 0, keepdims=True)
    return inv_std * (grad - first - normed * second)


def add_low(a, b):
    return (a.astype(F32) + b.astype(F32)).astype(BF)


G_OUT, G_IN, G_O, G_QKV = range(4)


def layer_kernel(dims, *refs):
    batch_count, seq_count, block_len, width, ff, fused = dims
    refs = list(refs)

    def take(count):
        taken = refs[:count]
        del refs[:count]
        return taken

    hidden_ref, cot_ref, len_ref, cot_pool_ref = take(4)
    vectors = take(9)
    w_qkv_hbm, w_o_hbm, w_in_hbm, w_out_hbm = take(4)
    out_ref, gin_ref, pooled_ref, vecs_ref = take(4)
    grad_refs = take(4)
    w_qkv, w_o, w_in, w_out = take(4)
    x_rows, cot_rows, x_t, qkv_t, expo, inv_sum, att_t = take(7)
    normed_one, middle_low, act, slope, normed_two, grad_second, low_a, grad_att = take(8)
    vec_cols, w_sem, own_sem = take(3)
    x_send, x_recv, c_send, c_recv, o_send, o_recv, g_send, g_recv = take(8)
    if fused:
        (send_core,) = take(1)
        held_core, held_one, held_two, held_z, z_one, z_two = (take(4) for _ in range(6))
        core_send, core_recv, link_send, link_recv = take(4)
        vec_own, vec_in, pool_own, pool_in, v_send, v_recv, p_send, p_recv = take(8)
    else:
        stage, put_sem = take(2)
    seq_len = seq_count * block_len
    head = width // H
    parts = ff // width
    me_b = lax.axis_index("batch")
    me_s = lax.axis_index("seq")

    loads = []
    for k, (src, dst) in enumerate(
        ((w_qkv_hbm, w_qkv), (w_o_hbm, w_o), (w_in_hbm, w_in), (w_out_hbm, w_out))
    ):
        load = pltpu.make_async_copy(src, dst, w_sem.at[k])
        load.start()
        loads.append(load)

    def flipped(index, bit):
        return index + bit - 2 * bit * lax.rem(index // bit, 2)

    def seq_peer(d):
        return (me_b, lax.rem(me_s + d, seq_count))

    core, at_x, at_y = lax.rem(me_b, 2), lax.rem(me_b // 2, 2), lax.rem(me_b // 4, 2)
    z_lo, z_hi = lax.rem(me_s, 2), lax.rem(me_s // 2, 2)
    to_core, to_x, to_y = ((flipped(me_b, bit), me_s) for bit in (1, 2, 4))
    to_z_lo, to_z_hi = ((me_b, flipped(me_s, bit)) for bit in (1, 2))

    barrier = pltpu.get_barrier_semaphore()
    greeted = [seq_peer(d) for d in range(1, seq_count)]
    if fused:
        greeted += [to_core, to_x, to_y]
    for device in greeted:
        pl.semaphore_signal(barrier, inc=1, device_id=device, device_id_type=MESH)
    pl.semaphore_wait(barrier, len(greeted))

    def remote(src, dst, device, send_sem, recv_sem):
        copy = pltpu.make_async_remote_copy(
            src_ref=src,
            dst_ref=dst,
            send_sem=send_sem,
            recv_sem=recv_sem,
            device_id=device,
            device_id_type=MESH,
        )
        copy.start()
        return copy

    def exchange(src, dst, own, send_sem, recv_sem):
        copies = []
        for d in range(1, seq_count):
            to = lax.rem(me_s + d, seq_count)
            copies.append(
                remote(src.at[to], dst.at[me_s], seq_peer(d), send_sem.at[d], recv_sem.at[d])
            )
        copy = pltpu.make_async_copy(src.at[me_s], dst.at[me_s], own_sem.at[own])
        copy.start()
        copies.append(copy)
        return copies

    def finish(copies):
        for copy in copies:
            copy.wait()

    hidden_copies = exchange(hidden_ref, x_rows, 0, x_send, x_recv)

    cot_pool = cot_pool_ref[...].astype(F32)
    is_mine = lax.broadcasted_iota(jnp.int32, cot_pool.shape, 0) == me_s
    cot_pool = jnp.sum(jnp.where(is_mine, cot_pool, 0.0), 0, keepdims=True)
    rows = [ref[...].astype(F32).reshape(1, width) for ref in vectors[:8]] + [cot_pool]
    for i in range(parts):
        rows.append(vectors[8][i * width : (i + 1) * width].astype(F32).reshape(1, width))
    rows.append(jnp.zeros((128 - len(rows), width), F32))
    vec_t = jnp.transpose(jnp.concatenate(rows, 0))
    vec_cols[...] = jnp.zeros((width, 128), F32)

    def column(index):
        return vec_t[:, index : index + 1]

    length = len_ref[me_s]
    inv_len = 1.0 / jnp.full((1, seq_len), length, jnp.int32).astype(F32)
    token_at = lax.broadcasted_iota(jnp.int32, (1, seq_len), 1)
    live = jnp.where(token_at < length, 1.0, 0.0).astype(F32)
    key_at = lax.broadcasted_iota(jnp.int32, (seq_len, 1), 0)
    key_bias = jnp.where(key_at < length, 0.0, -1e30).astype(F32)

    finish(hidden_copies)
    cot_copies = exchange(cot_ref, cot_rows, 1, c_send, c_recv)
    x_t[...] = jnp.transpose(x_rows[...].reshape(seq_len, width))

    loads[0].wait()
    scale = head ** (-0.5)
    qkv_t[0:width, :] = (
        (tn(w_qkv[:, 0:width], x_t[...]) + column(V_BQ)) * scale
    ).astype(BF)
    qkv_t[width : 2 * width, :] = tn(w_qkv[:, width : 2 * width], x_t[...]).astype(BF)
    qkv_t[2 * width :, :] = (tn(w_qkv[:, 2 * width :], x_t[...]) + column(V_BV)).astype(BF)

    def head_rows(h, third):
        return pl.ds(pl.multiple_of(h * head + third * width, head), head)

    def attend(h, carry):
        scores = tn(qkv_t[head_rows(h, 1), :], qkv_t[head_rows(h, 0), :]) + key_bias
        top = jnp.max(scores, 0, keepdims=True)
        weights = jnp.exp(scores - top)
        inverse = 1.0 / jnp.sum(weights, 0, keepdims=True)
        weights_low = weights.astype(BF)
        expo[aligned(h, seq_len), :] = weights_low
        inv_sum[aligned(h, 8), :] = jnp.broadcast_to(inverse, (8, seq_len))
        att_t[head_rows(h, 0), :] = (nn(qkv_t[head_rows(h, 2), :], weights_low) * inverse).astype(BF)
        return carry

    lax.fori_loop(0, H, attend, 0)

    loads[1].wait()
    summed = x_t[...].astype(F32) + (tn(w_o[...], att_t[...]) + column(V_BO))
    centred = summed - jnp.mean(summed, 0, keepdims=True)
    inv_one = lax.rsqrt(jnp.mean(centred * centred, 0, keepdims=True) + 1e-12)
    normed_one[...] = centred * inv_one
    middle_low[...] = (normed_one[...] * column(V_G1) + column(V_S1)).astype(BF)

    loads[2].wait()
    for i in range(parts):
        rows = slice(i * width, (i + 1) * width)
        pre = tn(w_in[:, rows], middle_low[...]) + column(V_BIN + i)
        cumulative = 0.5 * (1.0 + lax.erf(pre * 0.7071067811865476))
        density = jnp.exp(-0.5 * pre * pre) * 0.3989422804014327
        act[rows, :] = (pre * cumulative).astype(BF)
        slope[rows, :] = (cumulative + pre * density).astype(BF)
    loads[3].wait()
    middle = normed_one[...] * column(V_G1) + column(V_S1)
    summed = middle + (tn(w_out[...], act[...]) + column(V_BOUT))
    centred = summed - jnp.mean(summed, 0, keepdims=True)
    inv_two = lax.rsqrt(jnp.mean(centred * centred, 0, keepdims=True) + 1e-12)
    normed_two[...] = centred * inv_two
    finish(cot_copies)
    grad_final = jnp.transpose(cot_rows[...].reshape(seq_len, width)).astype(F32)
    grad_final = grad_final + column(V_CP) * (live * inv_len)
    grad_second[...] = norm_back(grad_final * column(V_G2), normed_two[...], inv_two)
    low_a[...] = grad_second[...].astype(BF)

    def whole_grad(m):
        if m == G_OUT:
            rows, columns = act, low_a
        elif m == G_IN:
            rows, columns = middle_low, slope
        elif m == G_O:
            rows, columns = att_t, low_a
        else:
            rows, columns = x_t, qkv_t
        return rows, columns

    def put(m):
        rows, columns = whole_grad(m)
        for i in range(rows.shape[0] // width):
            value = nt(rows[i * width : (i + 1) * width, :], columns[...])
            here = stage.at[:, 0 : value.shape[1]]
            here[...] = value.astype(BF)
            copy = pltpu.make_async_copy(
                here, grad_refs[m].at[i * width : (i + 1) * width, :], put_sem.at[0]
            )
            copy.start()
            copy.wait()

    flight = {}

    def partial(m, which):
        rows, columns = whole_grad(m)
        deep = rows.shape[0] // batch_count
        left = jnp.concatenate([rows[aligned(2 * j + which, deep), :] for j in range(4)], 0)
        tile = width // 2
        half = columns.shape[0] // 2
        for h in range(2):
            value = nt(left, columns[h * half : (h + 1) * half, :])
            for j in range(4):
                for t in range(half // tile):
                    block = value[j * deep : (j + 1) * deep, t * tile : (t + 1) * tile]
                    yield h, j, slice(t * deep, (t + 1) * deep), block

    def core_buffer(m):
        rows = held_core[m].shape[3]
        start = held_core[G_O].shape[3] if m == G_QKV else 0
        return send_core.at[:, :, :, start : start + rows, :]

    def core_start(m):
        buffer = core_buffer(m)
        if m == G_IN:
            for copy in flight[G_OUT, 0]:
                copy.wait_send()
        if m == G_O:
            for copy in flight[G_IN, 0]:
                copy.wait_send()
        for h, j, rows, block in partial(m, 1 - core):
            buffer[h, j // 2, j % 2, rows, :] = block.astype(BF)
        flight[m, 0] = [
            remote(buffer, held_core[m], to_core, core_send.at[m, 0], core_recv.at[m, 0])
        ]

    def core_add(m):
        for copy in flight[m, 0]:
            copy.wait_recv()
            if m in (G_O, G_QKV):
                copy.wait_send()
        held = held_core[m]
        for h, j, rows, block in partial(m, core):
            held[h, j // 2, j % 2, rows, :] = add_low(held[h, j // 2, j % 2, rows, :], block)

    def first_link(m):
        held = held_core[m]
        flight[m, 1] = [
            remote(
                held.at[0, :, 1 - at_x],
                held_one[m].at[0],
                to_x,
                link_send.at[m, 0],
                link_recv.at[m, 0],
            ),
            remote(
                held.at[1, 1 - at_y],
                held_one[m].at[1],
                to_y,
                link_send.at[m, 1],
                link_recv.at[m, 1],
            ),
        ]

    order = ((1 - at_y, 1 - at_x), (at_y, 1 - at_x), (1 - at_y, at_x), (at_y, at_x))

    def first_block(y, x, which):
        deep = ff // batch_count
        row = aligned(4 * y + 2 * x + which, deep)
        return nt(act[row, :], low_a[...])

    def first_start():
        buffer = send_core
        copies = []
        for k, (y, x) in enumerate(order):
            value = first_block(y, x, 1 - core)
            half = value.shape[1] // 2
            buffer[0, y, x] = value[:, :half].astype(BF)
            buffer[1, y, x] = value[:, half:].astype(BF)
            copies.append(
                remote(
                    buffer.at[:, y, x],
                    held_core[G_OUT].at[:, y, x],
                    to_core,
                    core_send.at[G_OUT, k],
                    core_recv.at[G_OUT, k],
                )
            )
        flight[G_OUT, 0] = copies

    def first_add():
        held, after = held_core[G_OUT], held_one[G_OUT]
        copies = []
        for k, (y, x) in enumerate(order):
            flight[G_OUT, 0][k].wait_recv()
            value = first_block(y, x, core)
            half = value.shape[1] // 2
            held[0, y, x] = add_low(held[0, y, x], value[:, :half])
            held[1, y, x] = add_low(held[1, y, x], value[:, half:])
            if k in (0, 1):
                copies.append(
                    remote(
                        held.at[0, y, x],
                        after.at[0, y],
                        to_x,
                        link_send.at[G_OUT, k],
                        link_recv.at[G_OUT, k],
                    )
                )
            if k in (0, 2):
                copies.append(
                    remote(
                        held.at[1, y, x],
                        after.at[1, x],
                        to_y,
                        link_send.at[G_OUT, 2 + k // 2],
                        link_recv.at[G_OUT, 2 + k // 2],
                    )
                )
        flight[G_OUT, 1] = copies

    def second_link(m):
        finish(flight[m, 1])
        held, after = held_core[m], held_one[m]
        after[0, 1 - at_y] = add_low(after[0, 1 - at_y], held[0, 1 - at_y, at_x])
        after[1, 1 - at_x] = add_low(after[1, 1 - at_x], held[1, at_y, 1 - at_x])
        flight[m, 2] = [
            remote(
                after.at[0, 1 - at_y],
                held_two[m].at[0],
                to_y,
                link_send.at[m, 4],
                link_recv.at[m, 4],
            ),
            remote(
                after.at[1, 1 - at_x],
                held_two[m].at[1],
                to_x,
                link_send.at[m, 5],
                link_recv.at[m, 5],
            ),
        ]
        after[0, at_y] = add_low(after[0, at_y], held[0, at_y, at_x])
        after[1, at_x] = add_low(after[1, at_x], held[1, at_y, at_x])

    def first_z(m):
        finish(flight[m, 2])
        after, last, ready = held_one[m], held_two[m], held_z[m]
        for h in range(2):
            mine = after[0, at_y] if h == 0 else after[1, at_x]
            block = last[h].astype(F32) + mine.astype(F32)
            if m == G_IN:
                deep = block.shape[0] // 2
                for k in range(2):
                    ready[h, k] = block[k * deep : (k + 1) * deep, :].astype(BF)
                continue
            deep = grad_refs[m].shape[0]
            per_row = width // 256
            count = block.shape[0] // deep * per_row
            tiles = []
            for t in range(count):
                row, lane = t // per_row * deep, t % per_row * 128
                tiles.append(block[row : row + deep, lane : lane + 128])
            full = count // 2
            for k in range(2):
                for t in range(full):
                    ready[h, k, t * deep : (t + 1) * deep, :] = tiles[t + k * (full + 1)].astype(BF)
            turned = pltpu.roll(tiles[full], 64, 1)
            left = lax.broadcasted_iota(jnp.int32, (deep // 2, 128), 1) < 64
            upper, lower = slice(0, deep // 2), slice(deep // 2, deep)
            folded = (
                jnp.where(left, tiles[full][upper], turned[lower]),
                jnp.where(left, turned[upper], tiles[full][lower]),
            )
            for k in range(2):
                ready[h, k, full * deep :, :] = folded[k].astype(BF)
        flight[m, 3] = [
            remote(
                ready.at[:, 1 - z_lo], z_one[m], to_z_lo, link_send.at[m, 6], link_recv.at[m, 6]
            )
        ]

    def second_z(m):
        finish(flight[m, 3])
        z_one[m][1 - z_hi] = add_low(z_one[m][1 - z_hi], held_z[m][1 - z_hi, z_lo])
        flight[m, 4] = [
            remote(
                z_one[m].at[1 - z_hi], z_two[m], to_z_hi, link_send.at[m, 7], link_recv.at[m, 7]
            )
        ]

    def last_sum(m):
        mine = z_one[m][z_hi].astype(F32) + held_z[m][z_hi, z_lo].astype(F32)
        finish(flight[m, 4])
        total = mine + z_two[m][...].astype(F32)
        out = grad_refs[m]
        deep, wide = out.shape
        if m == G_IN:
            out[:, : wide // 2] = total[:deep, :]
            out[:, wide // 2 :] = total[deep:, :]
            return
        full = wide // 128
        tiles = [total[t * deep : (t + 1) * deep, :] for t in range(full)]
        folded = total[full * deep :, :]
        turned = pltpu.roll(folded, 64, 1)
        after_tiles = jnp.concatenate(tiles + [jnp.concatenate([folded, turned], 0)], 1)
        before_tiles = jnp.concatenate([jnp.concatenate([turned, folded], 0)] + tiles, 1)
        before_tiles = pltpu.roll(before_tiles, full * 128 + 64, 1)
        out[...] = jnp.where(z_lo == 0, after_tiles, before_tiles)[:, :wide]

    peers = (to_core, to_x, to_y, to_z_lo, to_z_hi)

    def vector_start():
        vec_own[0] = jnp.transpose(vec_cols[...])[0:16, :]
        flight["v"] = remote(vec_own.at[0], vec_in.at[0], peers[0], v_send.at[0], v_recv.at[0])

    def vector_step(k):
        flight["v"].wait()
        total = vec_own[k] + vec_in[k]
        if k == 4:
            vecs_ref[...] = total
        else:
            vec_own[k + 1] = total
            flight["v"] = remote(
                vec_own.at[k + 1],
                vec_in.at[k + 1],
                peers[k + 1],
                v_send.at[k + 1],
                v_recv.at[k + 1],
            )

    if fused:
        first_start()
        first_add()
    else:
        put(G_OUT)

    rows_out = x_rows
    output = normed_two[...] * column(V_G2) + column(V_S2)
    rows_out[...] = jnp.transpose(output.astype(BF)).reshape(seq_count, block_len, width)
    out_copies = exchange(rows_out, out_ref, 2, o_send, o_recv)
    pooled_col = jnp.sum(output * (live * inv_len), 1, keepdims=True)
    if fused:
        pool_own[...] = jnp.transpose(jnp.broadcast_to(pooled_col, (width, 128)))[0:8, :]
        pool_in[me_s] = pool_own[...]
        flight["p"] = [
            remote(pool_own, pool_in.at[me_s], seq_peer(d), p_send.at[d], p_recv.at[d])
            for d in range(1, seq_count)
        ]
    else:
        vec_cols[:, 12:13] = pooled_col
    grad_final = jnp.transpose(cot_rows[...].reshape(seq_len, width)).astype(F32)
    grad_final = grad_final + column(V_CP) * (live * inv_len)
    vec_cols[:, 0:1] = jnp.sum(grad_final * normed_two[...], 1, keepdims=True)
    vec_cols[:, 1:2] = jnp.sum(grad_final, 1, keepdims=True)
    vec_cols[:, 2:3] = jnp.sum(low_a[...].astype(F32), 1, keepdims=True)

    for i in range(parts):
        rows = slice(i * width, (i + 1) * width)
        grad_act_low = nn(w_out[rows, :], low_a[...]).astype(BF)
        grad_pre = (grad_act_low.astype(F32) * slope[rows, :].astype(F32)).astype(BF)
        slope[rows, :] = grad_pre
        vec_cols[:, 3 + i : 4 + i] = jnp.sum(grad_pre.astype(F32), 1, keepdims=True)
    if fused:
        core_start(G_IN)
    else:
        put(G_IN)
    grad_middle = grad_second[...] + nn(w_in[...], slope[...])

    vec_cols[:, 7:8] = jnp.sum(grad_middle * normed_one[...], 1, keepdims=True)
    vec_cols[:, 8:9] = jnp.sum(grad_middle, 1, keepdims=True)
    grad_first = normed_two
    grad_first[...] = norm_back(grad_middle * column(V_G1), normed_one[...], inv_one)
    low_a[...] = grad_first[...].astype(BF)
    vec_cols[:, 9:10] = jnp.sum(low_a[...].astype(F32), 1, keepdims=True)
    if fused:
        second_link(G_OUT)
        core_add(G_IN)
        first_link(G_IN)
        core_start(G_O)
    else:
        put(G_O)
    grad_heads = nn(w_o[...], low_a[...])
    for h in range(H):
        rows = slice(h * head, (h + 1) * head)
        grad_att[rows, :] = (grad_heads[rows, :] * inv_sum[h * 8 : h * 8 + 1, :]).astype(BF)
    if fused:
        core_add(G_O)

    def attend_back(h, carry):
        grad = grad_att[head_rows(h, 0), :]
        inner = jnp.sum(grad.astype(F32) * att_t[head_rows(h, 0), :].astype(F32), 0, keepdims=True)
        weights_low = expo[aligned(h, seq_len), :]
        queries, keys, values = (qkv_t[head_rows(h, third), :] for third in range(3))
        grad_probs = tn(values, grad)
        grad_scores = (weights_low.astype(F32) * (grad_probs - inner)).astype(BF)
        qkv_t[head_rows(h, 0), :] = (nn(keys, grad_scores) * scale).astype(BF)
        qkv_t[head_rows(h, 1), :] = nt(queries, grad_scores).astype(BF)
        qkv_t[head_rows(h, 2), :] = nt(grad, weights_low).astype(BF)
        return carry

    if fused:
        for k in range(3):
            lax.fori_loop(k * (H // 3), (k + 1) * (H // 3), attend_back, 0)
            if k == 0:
                first_z(G_OUT)
            if k == 2:
                second_z(G_OUT)
    else:
        lax.fori_loop(0, H, attend_back, 0)
    vec_cols[:, 10:11] = jnp.sum(qkv_t[0:width, :].astype(F32), 1, keepdims=True)
    vec_cols[:, 11:12] = jnp.sum(qkv_t[2 * width :, :].astype(F32), 1, keepdims=True)
    if fused:
        vector_start()
        core_start(G_QKV)
    grad_in = nn(w_qkv[...], qkv_t[...]) + grad_first[...]
    rows_gin = cot_rows
    rows_gin[...] = jnp.transpose(grad_in.astype(BF)).reshape(seq_count, block_len, width)
    gin_copies = exchange(rows_gin, gin_ref, 3, g_send, g_recv)
    if fused:
        core_add(G_QKV)
        second_link(G_IN)
        vector_step(0)
        first_link(G_QKV)
        first_link(G_O)
        first_z(G_IN)
        last_sum(G_OUT)
        vector_step(1)
        second_link(G_QKV)
        second_link(G_O)
        second_z(G_IN)
        vector_step(2)
        first_z(G_QKV)
        first_z(G_O)
        last_sum(G_IN)
        vector_step(3)
        second_z(G_QKV)
        second_z(G_O)
        finish(flight["p"])
        for k in range(seq_count):
            pooled_ref[k : k + 1, :] = pool_in[k, 0:1, :]
        vector_step(4)
        last_sum(G_QKV)
        last_sum(G_O)
    else:
        put(G_QKV)
        vecs_ref[...] = jnp.transpose(vec_cols[...])[0:16, :]
        pooled_ref[...] = jnp.transpose(vec_cols[...])[12:16, :]
    finish(out_copies)
    finish(gin_copies)


def deliver_kernel(*refs):
    out_in, gin_in, pooled_in, vecs_in = refs[:4]
    grads_in = refs[4:8]
    out_ref, gin_ref, pooled_ref = refs[8:11]
    grad_refs, vec_refs = refs[11:15], refs[15:24]
    grad_refs[0][...] = jnp.transpose(grads_in[0][...])
    moves = [(out_in, out_ref), (gin_in, gin_ref), (pooled_in, pooled_ref)]
    for src, dst in moves + list(zip(grads_in[1:], grad_refs[1:])):
        dst[...] = src[...]
    width = vecs_in.shape[1]
    for row, ref in zip((10, 11, 9, 7, 8, 3, 2, 0, 1), vec_refs):
        for i in range(ref.shape[0] // width):
            ref[i * width : (i + 1) * width] = vecs_in[row + i : row + i + 1, :].reshape(width)


def deliver(outs):
    out_hidden, grad_in, pooled, total, g_out, g_in, g_o, g_qkv = outs
    ff = total.shape[1] * g_out.shape[0] // g_qkv.shape[0]
    vmem = pl.BlockSpec(memory_space=pltpu.VMEM)
    arrays = (out_hidden, grad_in, pooled, g_out, g_in, g_o, g_qkv)
    lengths = [total.shape[1]] * 5 + [ff] + [total.shape[1]] * 3
    vectors = tuple(jax.ShapeDtypeStruct((n,), F32) for n in lengths)
    shapes = [jax.ShapeDtypeStruct(a.shape, a.dtype) for a in arrays]
    shapes[3] = jax.ShapeDtypeStruct(g_out.shape[::-1], F32)
    results = pl.pallas_call(
        deliver_kernel,
        out_shape=tuple(shapes) + vectors,
        in_specs=[vmem] * 8,
        out_specs=(vmem,) * 16,
        name="deliver",
    )(*outs)
    out_hidden, grad_in, pooled, g_out, g_in, g_o, g_qkv = results[:7]
    b_q, b_v, b_o, gain_one, shift_one, b_in, b_out, gain_two, shift_two = results[7:]
    return (
        out_hidden,
        pooled,
        grad_in,
        g_qkv,
        b_q,
        b_v,
        g_o,
        b_o,
        gain_one,
        shift_one,
        g_in,
        b_in,
        g_out.T,
        b_out,
        gain_two,
        shift_two,
    )


def body(
    hidden_in,
    lengths,
    w_qkv,
    b_q,
    b_v,
    w_o,
    b_o,
    gain_one,
    shift_one,
    w_in,
    b_in,
    w_out,
    b_out,
    gain_two,
    shift_two,
    cot_hidden,
    cot_pooled,
):
    batch_count, seq_count = lax.axis_size("batch"), lax.axis_size("seq")
    seqs_here, block_len, width = hidden_in.shape
    ff = w_in.shape[1]
    seq_len = seq_count * block_len
    assert seqs_here == seq_count
    fused = batch_count == 8 and seq_count == 4

    anywhere = pl.BlockSpec(memory_space=pl.ANY)
    vmem = pl.BlockSpec(memory_space=pltpu.VMEM)
    smem = pl.BlockSpec(memory_space=pltpu.SMEM)
    rows = jax.ShapeDtypeStruct(hidden_in.shape, BF)
    weights = (w_out, w_in, w_o, w_qkv)
    if fused:
        grads = tuple(
            jax.ShapeDtypeStruct((w.shape[0] // batch_count, w.shape[1] // seq_count), F32)
            for w in weights
        )
    else:
        grads = tuple(jax.ShapeDtypeStruct(w.shape, BF) for w in weights)
    dma = pltpu.SemaphoreType.DMA
    scratch = [pltpu.VMEM(w.shape, BF) for w in (w_qkv, w_o, w_in, w_out)]
    scratch += [
        pltpu.VMEM((seq_count, block_len, width), BF),
        pltpu.VMEM((seq_count, block_len, width), BF),
        pltpu.VMEM((width, seq_len), BF),
        pltpu.VMEM((3 * width, seq_len), BF),
        pltpu.VMEM((H * seq_len, seq_len), BF),
        pltpu.VMEM((H * 8, seq_len), F32),
        pltpu.VMEM((width, seq_len), BF),
        pltpu.VMEM((width, seq_len), F32),
        pltpu.VMEM((width, seq_len), BF),
        pltpu.VMEM((ff, seq_len), BF),
        pltpu.VMEM((ff, seq_len), BF),
        pltpu.VMEM((width, seq_len), F32),
        pltpu.VMEM((width, seq_len), F32),
        pltpu.VMEM((width, seq_len), BF),
        pltpu.VMEM((width, seq_len), BF),
        pltpu.VMEM((width, 128), F32),
        dma((4,)),
        dma((4,)),
    ]
    scratch += [dma((seq_count,))] * 8
    if fused:
        deep = width // batch_count
        blocks = (
            (ff // batch_count, width // 2),
            (deep * (ff // width), width // 2),
            (deep, width // 2),
            (deep * 3, width // 2),
        )
        z_blocks = tuple(
            (block[0] // 2, block[1]) if m == G_IN else (block[0] * block[1] // 256, 128)
            for m, block in enumerate(blocks)
        )
        scratch += [pltpu.VMEM((2, 2, 2) + blocks[0], BF)]
        scratch += [pltpu.VMEM((2, 2, 2) + block, BF) for block in blocks]
        scratch += [pltpu.VMEM((2, 2) + block, BF) for block in blocks]
        scratch += [pltpu.VMEM((2,) + block, BF) for block in blocks]
        scratch += [pltpu.VMEM((2, 2) + block, BF) for block in z_blocks]
        scratch += [pltpu.VMEM((2,) + block, BF) for block in z_blocks]
        scratch += [pltpu.VMEM(block, BF) for block in z_blocks]
        scratch += [dma((4, 4)), dma((4, 4)), dma((4, 8)), dma((4, 8))]
        scratch += [
            pltpu.VMEM((5, 16, width), F32),
            pltpu.VMEM((5, 16, width), F32),
            pltpu.VMEM((8, width), F32),
            pltpu.VMEM((seq_count, 8, width), F32),
            dma((5,)),
            dma((5,)),
            dma((seq_count,)),
            dma((seq_count,)),
        ]
    else:
        scratch += [pltpu.VMEM((width, ff), BF), dma((1,))]
    outs = pl.pallas_call(
        functools.partial(
            layer_kernel, (batch_count, seq_count, block_len, width, ff, fused)
        ),
        out_shape=(
            rows,
            rows,
            jax.ShapeDtypeStruct((seq_count, width), F32),
            jax.ShapeDtypeStruct((16, width), F32),
        )
        + grads,
        in_specs=[anywhere, anywhere, smem] + [vmem] * 10 + [anywhere] * 4,
        out_specs=(anywhere, anywhere, vmem, vmem) + (vmem if fused else anywhere,) * 4,
        scratch_shapes=scratch,
        compiler_params=pltpu.CompilerParams(
            collective_id=0, has_side_effects=True, vmem_limit_bytes=63 * 2**20
        ),
        name="encoder_layer",
    )(
        hidden_in,
        cot_hidden,
        lengths,
        cot_pooled,
        b_q,
        b_v,
        b_o,
        gain_one,
        shift_one,
        b_out,
        gain_two,
        shift_two,
        b_in,
        w_qkv,
        w_o,
        w_in,
        w_out,
    )
    if fused:
        return deliver(outs)
    out_hidden, grad_in, pooled, total, g_out, g_in, g_o, g_qkv = outs
    pooled = lax.all_gather(pooled[0], "seq", axis=0)
    total = lax.psum(total[:12], ("batch", "seq"))

    def scatter(grad):
        part = lax.psum_scatter(grad.astype(F32), "batch", scatter_dimension=0, tiled=True)
        part = lax.psum_scatter(part.astype(BF), "seq", scatter_dimension=1, tiled=True)
        return part.astype(F32)

    g_out, g_in, g_o, g_qkv = (scatter(g) for g in (g_out, g_in, g_o, g_qkv))
    return (
        out_hidden,
        pooled,
        grad_in,
        g_qkv,
        total[10],
        total[11],
        g_o,
        total[9],
        total[7],
        total[8],
        g_in,
        total[3:7].reshape(ff),
        g_out,
        total[2],
        total[0],
        total[1],
    )


def solution(mesh):
    rows = P("batch", "seq", None)
    shard = P("batch", "seq")
    in_specs = (rows, P("batch")) + (P(),) * 13 + (rows, P("batch", None))
    out_specs = (
        rows,
        P("batch", None),
        rows,
        shard,
        P(),
        P(),
        shard,
        P(),
        P(),
        P(),
        shard,
        P(),
        shard,
        P(),
        P(),
        P(),
    )
    return jax.shard_map(body, mesh=mesh, in_specs=in_specs, out_specs=out_specs, check_vma=False)
```

```python
import functools

import jax
import jax.numpy as jnp
from jax import lax
from jax.experimental import pallas as pl
from jax.experimental.pallas import tpu as pltpu
from jax.sharding import PartitionSpec as P

H = 12
BF = jnp.bfloat16
F32 = jnp.float32
MESH = pl.DeviceIdType.MESH
V_BQ, V_BV, V_BO, V_G1, V_S1, V_BOUT, V_G2, V_S2, V_CP, V_BIN = range(10)


def nn(a, b):
    return lax.dot_general(a, b, (((1,), (0,)), ((), ())), preferred_element_type=F32)


def nt(a, b):
    return lax.dot_general(a, b, (((1,), (1,)), ((), ())), preferred_element_type=F32)


def tn(a, b):
    return lax.dot_general(a, b, (((0,), (0,)), ((), ())), preferred_element_type=F32)


def aligned(index, size):
    return pl.ds(pl.multiple_of(index * size, size), size)


def norm_back(grad, normed, inv_std):
    first = jnp.mean(grad, 0, keepdims=True)
    second = jnp.mean(grad * normed, 0, keepdims=True)
    return inv_std * (grad - first - normed * second)


def add_low(a, b):
    return (a.astype(F32) + b.astype(F32)).astype(BF)


G_OUT, G_IN, G_O, G_QKV = range(4)


def layer_kernel(dims, *refs):
    batch_count, seq_count, block_len, width, ff, fused = dims
    refs = list(refs)

    def take(count):
        taken = refs[:count]
        del refs[:count]
        return taken

    hidden_ref, cot_ref, len_ref, cot_pool_ref = take(4)
    vectors = take(9)
    w_qkv_hbm, w_o_hbm, w_in_hbm, w_out_hbm = take(4)
    out_ref, gin_ref, pooled_ref, vecs_ref = take(4)
    grad_refs = take(4)
    w_qkv, w_o, w_in, w_out = take(4)
    x_rows, cot_rows, x_t, qkv_t, expo, inv_sum, att_t = take(7)
    normed_one, middle_low, act, slope, normed_two, low_a, grad_att = take(7)
    vec_cols, w_sem, own_sem = take(3)
    x_send, x_recv, c_send, c_recv, o_send, o_recv, g_send, g_recv = take(8)
    if fused:
        (send_core,) = take(1)
        held_core, held_one, held_two, held_z, z_one, z_two = (take(4) for _ in range(6))
        core_send, core_recv, link_send, link_recv = take(4)
        vec_own, vec_in, pool_own, pool_in, v_send, v_recv, p_send, p_recv = take(8)
    else:
        stage, put_sem = take(2)
    seq_len = seq_count * block_len
    head = width // H
    parts = ff // width
    me_b = lax.axis_index("batch")
    me_s = lax.axis_index("seq")

    loads = []
    for k, (src, dst) in enumerate(
        ((w_qkv_hbm, w_qkv), (w_o_hbm, w_o), (w_in_hbm, w_in), (w_out_hbm, w_out))
    ):
        load = pltpu.make_async_copy(src, dst, w_sem.at[k])
        load.start()
        loads.append(load)

    def flipped(index, bit):
        return index + bit - 2 * bit * lax.rem(index // bit, 2)

    def seq_peer(d):
        return (me_b, lax.rem(me_s + d, seq_count))

    core, at_x, at_y = lax.rem(me_b, 2), lax.rem(me_b // 2, 2), lax.rem(me_b // 4, 2)
    z_lo, z_hi = lax.rem(me_s, 2), lax.rem(me_s // 2, 2)
    to_core, to_x, to_y = ((flipped(me_b, bit), me_s) for bit in (1, 2, 4))
    to_z_lo, to_z_hi = ((me_b, flipped(me_s, bit)) for bit in (1, 2))

    barrier = pltpu.get_barrier_semaphore()
    greeted = [seq_peer(d) for d in range(1, seq_count)]
    if fused:
        greeted += [to_core, to_x, to_y]
    for device in greeted:
        pl.semaphore_signal(barrier, inc=1, device_id=device, device_id_type=MESH)
    pl.semaphore_wait(barrier, len(greeted))

    def remote(src, dst, device, send_sem, recv_sem):
        copy = pltpu.make_async_remote_copy(
            src_ref=src,
            dst_ref=dst,
            send_sem=send_sem,
            recv_sem=recv_sem,
            device_id=device,
            device_id_type=MESH,
        )
        copy.start()
        return copy

    def exchange(src, dst, own, send_sem, recv_sem):
        copies = []
        for d in range(1, seq_count):
            to = lax.rem(me_s + d, seq_count)
            copies.append(
                remote(src.at[to], dst.at[me_s], seq_peer(d), send_sem.at[d], recv_sem.at[d])
            )
        copy = pltpu.make_async_copy(src.at[me_s], dst.at[me_s], own_sem.at[own])
        copy.start()
        copies.append(copy)
        return copies

    def finish(copies):
        for copy in copies:
            copy.wait()

    hidden_copies = exchange(hidden_ref, x_rows, 0, x_send, x_recv)

    cot_pool = cot_pool_ref[...].astype(F32)
    is_mine = lax.broadcasted_iota(jnp.int32, cot_pool.shape, 0) == me_s
    cot_pool = jnp.sum(jnp.where(is_mine, cot_pool, 0.0), 0, keepdims=True)
    rows = [ref[...].astype(F32).reshape(1, width) for ref in vectors[:8]] + [cot_pool]
    for i in range(parts):
        rows.append(vectors[8][i * width : (i + 1) * width].astype(F32).reshape(1, width))
    rows.append(jnp.zeros((128 - len(rows), width), F32))
    vec_t = jnp.transpose(jnp.concatenate(rows, 0))
    vec_cols[...] = jnp.zeros((width, 128), F32)

    def column(index):
        return vec_t[:, index : index + 1]

    length = len_ref[me_s]
    inv_len = 1.0 / jnp.full((1, seq_len), length, jnp.int32).astype(F32)
    token_at = lax.broadcasted_iota(jnp.int32, (1, seq_len), 1)
    live = jnp.where(token_at < length, 1.0, 0.0).astype(F32)
    key_at = lax.broadcasted_iota(jnp.int32, (seq_len, 1), 0)
    key_bias = jnp.where(key_at < length, 0.0, -1e30).astype(F32)

    finish(hidden_copies)
    cot_copies = exchange(cot_ref, cot_rows, 1, c_send, c_recv)
    x_t[...] = jnp.transpose(x_rows[...].reshape(seq_len, width))

    loads[0].wait()
    scale = head ** (-0.5)
    qkv_t[0:width, :] = (
        (tn(w_qkv[:, 0:width], x_t[...]) + column(V_BQ)) * scale
    ).astype(BF)
    qkv_t[width : 2 * width, :] = tn(w_qkv[:, width : 2 * width], x_t[...]).astype(BF)
    qkv_t[2 * width :, :] = (tn(w_qkv[:, 2 * width :], x_t[...]) + column(V_BV)).astype(BF)

    def head_rows(h, third):
        return pl.ds(pl.multiple_of(h * head + third * width, head), head)

    def attend(h, carry):
        scores = tn(qkv_t[head_rows(h, 1), :], qkv_t[head_rows(h, 0), :]) + key_bias
        top = jnp.max(scores, 0, keepdims=True)
        weights = jnp.exp(scores - top)
        inverse = 1.0 / jnp.sum(weights, 0, keepdims=True)
        weights_low = weights.astype(BF)
        expo[aligned(h, seq_len), :] = weights_low
        inv_sum[aligned(h, 8), :] = jnp.broadcast_to(inverse, (8, seq_len))
        att_t[head_rows(h, 0), :] = (nn(qkv_t[head_rows(h, 2), :], weights_low) * inverse).astype(BF)
        return carry

    lax.fori_loop(0, H, attend, 0)

    loads[1].wait()
    summed = x_t[...].astype(F32) + (tn(w_o[...], att_t[...]) + column(V_BO))
    centred = summed - jnp.mean(summed, 0, keepdims=True)
    inv_one = lax.rsqrt(jnp.mean(centred * centred, 0, keepdims=True) + 1e-12)
    normed_one[...] = centred * inv_one
    middle_low[...] = (normed_one[...] * column(V_G1) + column(V_S1)).astype(BF)

    loads[2].wait()
    for i in range(parts):
        rows = slice(i * width, (i + 1) * width)
        pre = tn(w_in[:, rows], middle_low[...]) + column(V_BIN + i)
        cumulative = 0.5 * (1.0 + lax.erf(pre * 0.7071067811865476))
        density = jnp.exp(-0.5 * pre * pre) * 0.3989422804014327
        act[rows, :] = (pre * cumulative).astype(BF)
        slope[rows, :] = (cumulative + pre * density).astype(BF)
    loads[3].wait()
    middle = normed_one[...] * column(V_G1) + column(V_S1)
    summed = middle + (tn(w_out[...], act[...]) + column(V_BOUT))
    centred = summed - jnp.mean(summed, 0, keepdims=True)
    inv_two = lax.rsqrt(jnp.mean(centred * centred, 0, keepdims=True) + 1e-12)
    normed_two[...] = centred * inv_two
    finish(cot_copies)
    grad_final = jnp.transpose(cot_rows[...].reshape(seq_len, width)).astype(F32)
    grad_final = grad_final + column(V_CP) * (live * inv_len)
    low_a[...] = norm_back(grad_final * column(V_G2), normed_two[...], inv_two).astype(BF)

    def whole_grad(m):
        if m == G_OUT:
            rows, columns = act, low_a
        elif m == G_IN:
            rows, columns = middle_low, slope
        elif m == G_O:
            rows, columns = att_t, low_a
        else:
            rows, columns = x_t, qkv_t
        return rows, columns

    def put(m):
        rows, columns = whole_grad(m)
        for i in range(rows.shape[0] // width):
            value = nt(rows[i * width : (i + 1) * width, :], columns[...])
            here = stage.at[:, 0 : value.shape[1]]
            here[...] = value.astype(BF)
            copy = pltpu.make_async_copy(
                here, grad_refs[m].at[i * width : (i + 1) * width, :], put_sem.at[0]
            )
            copy.start()
            copy.wait()

    flight = {}

    def partial(m, which):
        rows, columns = whole_grad(m)
        deep = rows.shape[0] // batch_count
        left = jnp.concatenate([rows[aligned(2 * j + which, deep), :] for j in range(4)], 0)
        tile = width // 2
        half = columns.shape[0] // 2
        for h in range(2):
            value = nt(left, columns[h * half : (h + 1) * half, :])
            for j in range(4):
                for t in range(half // tile):
                    block = value[j * deep : (j + 1) * deep, t * tile : (t + 1) * tile]
                    yield h, j, slice(t * deep, (t + 1) * deep), block

    def core_buffer(m):
        rows = held_core[m].shape[3]
        start = held_core[G_O].shape[3] if m == G_QKV else 0
        return send_core.at[:, :, :, start : start + rows, :]

    def core_start(m):
        buffer = core_buffer(m)
        if m == G_IN:
            for copy in flight[G_OUT, 0]:
                copy.wait_send()
        if m == G_O:
            for copy in flight[G_IN, 0]:
                copy.wait_send()
        for h, j, rows, block in partial(m, 1 - core):
            buffer[h, j // 2, j % 2, rows, :] = block.astype(BF)
        flight[m, 0] = [
            remote(buffer, held_core[m], to_core, core_send.at[m, 0], core_recv.at[m, 0])
        ]

    def core_add(m):
        for copy in flight[m, 0]:
            copy.wait_recv()
            if m in (G_O, G_QKV):
                copy.wait_send()
        held = held_core[m]
        for h, j, rows, block in partial(m, core):
            held[h, j // 2, j % 2, rows, :] = add_low(held[h, j // 2, j % 2, rows, :], block)

    def first_link(m):
        held = held_core[m]
        flight[m, 1] = [
            remote(
                held.at[0, :, 1 - at_x],
                held_one[m].at[0],
                to_x,
                link_send.at[m, 0],
                link_recv.at[m, 0],
            ),
            remote(
                held.at[1, 1 - at_y],
                held_one[m].at[1],
                to_y,
                link_send.at[m, 1],
                link_recv.at[m, 1],
            ),
        ]

    order = ((1 - at_y, 1 - at_x), (at_y, 1 - at_x), (1 - at_y, at_x), (at_y, at_x))

    def first_block(y, x, which):
        deep = ff // batch_count
        row = aligned(4 * y + 2 * x + which, deep)
        return nt(act[row, :], low_a[...])

    def first_send(k):
        y, x = order[k]
        value = first_block(y, x, 1 - core)
        half = value.shape[1] // 2
        send_core[0, y, x] = value[:, :half].astype(BF)
        send_core[1, y, x] = value[:, half:].astype(BF)
        flight[G_OUT, 0].append(
            remote(
                send_core.at[:, y, x],
                held_core[G_OUT].at[:, y, x],
                to_core,
                core_send.at[G_OUT, k],
                core_recv.at[G_OUT, k],
            )
        )

    def first_add(k):
        held, after = held_core[G_OUT], held_one[G_OUT]
        y, x = order[k]
        value = first_block(y, x, core)
        half = value.shape[1] // 2
        flight[G_OUT, 0][k].wait_recv()
        held[0, y, x] = add_low(held[0, y, x], value[:, :half])
        held[1, y, x] = add_low(held[1, y, x], value[:, half:])
        hops = []
        if k in (0, 1):
            hops.append((0, after.at[0, y], to_x, k))
        if k in (0, 2):
            hops.append((1, after.at[1, x], to_y, 2 + k // 2))
        for h, dst, device, sem in hops:
            flight[G_OUT, 1].append(
                remote(
                    held.at[h, y, x],
                    dst,
                    device,
                    link_send.at[G_OUT, sem],
                    link_recv.at[G_OUT, sem],
                )
            )

    def first_sums():
        flight[G_OUT, 0], flight[G_OUT, 1] = [], []
        first_send(0)
        first_send(1)
        first_add(0)
        first_send(2)
        first_send(3)
        for k in range(1, 4):
            first_add(k)

    def second_link(m):
        finish(flight[m, 1])
        held, after = held_core[m], held_one[m]
        after[0, 1 - at_y] = add_low(after[0, 1 - at_y], held[0, 1 - at_y, at_x])
        after[1, 1 - at_x] = add_low(after[1, 1 - at_x], held[1, at_y, 1 - at_x])
        flight[m, 2] = [
            remote(
                after.at[0, 1 - at_y],
                held_two[m].at[0],
                to_y,
                link_send.at[m, 4],
                link_recv.at[m, 4],
            ),
            remote(
                after.at[1, 1 - at_x],
                held_two[m].at[1],
                to_x,
                link_send.at[m, 5],
                link_recv.at[m, 5],
            ),
        ]
        after[0, at_y] = add_low(after[0, at_y], held[0, at_y, at_x])
        after[1, at_x] = add_low(after[1, at_x], held[1, at_y, at_x])

    def first_z(m):
        finish(flight[m, 2])
        after, last, ready = held_one[m], held_two[m], held_z[m]
        for h in range(2):
            mine = after[0, at_y] if h == 0 else after[1, at_x]
            block = last[h].astype(F32) + mine.astype(F32)
            if m == G_IN:
                deep = block.shape[0] // 2
                for k in range(2):
                    ready[h, k] = block[k * deep : (k + 1) * deep, :].astype(BF)
                continue
            deep = grad_refs[m].shape[0]
            per_row = width // 256
            count = block.shape[0] // deep * per_row
            tiles = []
            for t in range(count):
                row, lane = t // per_row * deep, t % per_row * 128
                tiles.append(block[row : row + deep, lane : lane + 128])
            full = count // 2
            for k in range(2):
                for t in range(full):
                    ready[h, k, t * deep : (t + 1) * deep, :] = tiles[t + k * (full + 1)].astype(BF)
            turned = pltpu.roll(tiles[full], 64, 1)
            left = lax.broadcasted_iota(jnp.int32, (deep // 2, 128), 1) < 64
            upper, lower = slice(0, deep // 2), slice(deep // 2, deep)
            folded = (
                jnp.where(left, tiles[full][upper], turned[lower]),
                jnp.where(left, turned[upper], tiles[full][lower]),
            )
            for k in range(2):
                ready[h, k, full * deep :, :] = folded[k].astype(BF)
        flight[m, 3] = [
            remote(
                ready.at[:, 1 - z_lo], z_one[m], to_z_lo, link_send.at[m, 6], link_recv.at[m, 6]
            )
        ]

    def second_z(m):
        finish(flight[m, 3])
        z_one[m][1 - z_hi] = add_low(z_one[m][1 - z_hi], held_z[m][1 - z_hi, z_lo])
        flight[m, 4] = [
            remote(
                z_one[m].at[1 - z_hi], z_two[m], to_z_hi, link_send.at[m, 7], link_recv.at[m, 7]
            )
        ]

    def last_sum(m):
        mine = z_one[m][z_hi].astype(F32) + held_z[m][z_hi, z_lo].astype(F32)
        finish(flight[m, 4])
        total = mine + z_two[m][...].astype(F32)
        out = grad_refs[m]
        deep, wide = out.shape
        if m == G_IN:
            out[:, : wide // 2] = total[:deep, :]
            out[:, wide // 2 :] = total[deep:, :]
            return
        full = wide // 128
        tiles = [total[t * deep : (t + 1) * deep, :] for t in range(full)]
        folded = total[full * deep :, :]
        turned = pltpu.roll(folded, 64, 1)
        after_tiles = jnp.concatenate(tiles + [jnp.concatenate([folded, turned], 0)], 1)
        before_tiles = jnp.concatenate([jnp.concatenate([turned, folded], 0)] + tiles, 1)
        before_tiles = pltpu.roll(before_tiles, full * 128 + 64, 1)
        out[...] = jnp.where(z_lo == 0, after_tiles, before_tiles)[:, :wide]

    peers = (to_core, to_x, to_y, to_z_lo, to_z_hi)

    def vector_start():
        vec_own[0] = jnp.transpose(vec_cols[...])[0:16, :]
        flight["v"] = remote(vec_own.at[0], vec_in.at[0], peers[0], v_send.at[0], v_recv.at[0])

    def vector_step(k):
        flight["v"].wait()
        total = vec_own[k] + vec_in[k]
        if k == 4:
            vecs_ref[...] = total
        else:
            vec_own[k + 1] = total
            flight["v"] = remote(
                vec_own.at[k + 1],
                vec_in.at[k + 1],
                peers[k + 1],
                v_send.at[k + 1],
                v_recv.at[k + 1],
            )

    if fused:
        first_sums()
    else:
        put(G_OUT)

    rows_out = x_rows
    output = normed_two[...] * column(V_G2) + column(V_S2)
    rows_out[...] = jnp.transpose(output.astype(BF)).reshape(seq_count, block_len, width)
    out_copies = exchange(rows_out, out_ref, 2, o_send, o_recv)
    pooled_col = jnp.sum(output * (live * inv_len), 1, keepdims=True)
    if fused:
        pool_own[...] = jnp.transpose(jnp.broadcast_to(pooled_col, (width, 128)))[0:8, :]
        pool_in[me_s] = pool_own[...]
        flight["p"] = [
            remote(pool_own, pool_in.at[me_s], seq_peer(d), p_send.at[d], p_recv.at[d])
            for d in range(1, seq_count)
        ]
    else:
        vec_cols[:, 12:13] = pooled_col
    grad_final = jnp.transpose(cot_rows[...].reshape(seq_len, width)).astype(F32)
    grad_final = grad_final + column(V_CP) * (live * inv_len)
    vec_cols[:, 0:1] = jnp.sum(grad_final * normed_two[...], 1, keepdims=True)
    vec_cols[:, 1:2] = jnp.sum(grad_final, 1, keepdims=True)
    vec_cols[:, 2:3] = jnp.sum(low_a[...].astype(F32), 1, keepdims=True)

    for i in range(parts):
        rows = slice(i * width, (i + 1) * width)
        grad_act_low = nn(w_out[rows, :], low_a[...]).astype(BF)
        grad_pre = (grad_act_low.astype(F32) * slope[rows, :].astype(F32)).astype(BF)
        slope[rows, :] = grad_pre
        vec_cols[:, 3 + i : 4 + i] = jnp.sum(grad_pre.astype(F32), 1, keepdims=True)
    if fused:
        core_start(G_IN)
    else:
        put(G_IN)
    grad_middle = low_a[...].astype(F32) + nn(w_in[...], slope[...])
    if fused:
        second_link(G_OUT)

    vec_cols[:, 7:8] = jnp.sum(grad_middle * normed_one[...], 1, keepdims=True)
    vec_cols[:, 8:9] = jnp.sum(grad_middle, 1, keepdims=True)
    grad_first = normed_two
    grad_first[...] = norm_back(grad_middle * column(V_G1), normed_one[...], inv_one)
    low_a[...] = grad_first[...].astype(BF)
    vec_cols[:, 9:10] = jnp.sum(low_a[...].astype(F32), 1, keepdims=True)
    if fused:
        core_add(G_IN)
        first_link(G_IN)
        core_start(G_O)
    else:
        put(G_O)
    grad_heads = nn(w_o[...], low_a[...])
    for h in range(H):
        rows = slice(h * head, (h + 1) * head)
        grad_att[rows, :] = (grad_heads[rows, :] * inv_sum[h * 8 : h * 8 + 1, :]).astype(BF)
    if fused:
        core_add(G_O)

    def attend_back(h, carry):
        grad = grad_att[head_rows(h, 0), :]
        inner = jnp.sum(grad.astype(F32) * att_t[head_rows(h, 0), :].astype(F32), 0, keepdims=True)
        weights_low = expo[aligned(h, seq_len), :]
        queries, keys, values = (qkv_t[head_rows(h, third), :] for third in range(3))
        grad_probs = tn(values, grad)
        grad_scores = (weights_low.astype(F32) * (grad_probs - inner)).astype(BF)
        qkv_t[head_rows(h, 0), :] = (nn(keys, grad_scores) * scale).astype(BF)
        qkv_t[head_rows(h, 1), :] = nt(queries, grad_scores).astype(BF)
        qkv_t[head_rows(h, 2), :] = nt(grad, weights_low).astype(BF)
        return carry

    if fused:
        for k in range(3):
            lax.fori_loop(k * (H // 3), (k + 1) * (H // 3), attend_back, 0)
            if k == 0:
                first_z(G_OUT)
    else:
        lax.fori_loop(0, H, attend_back, 0)
    vec_cols[:, 10:11] = jnp.sum(qkv_t[0:width, :].astype(F32), 1, keepdims=True)
    vec_cols[:, 11:12] = jnp.sum(qkv_t[2 * width :, :].astype(F32), 1, keepdims=True)
    if fused:
        vector_start()
        core_start(G_QKV)
    grad_in = nn(w_qkv[...], qkv_t[...]) + grad_first[...]
    rows_gin = cot_rows
    rows_gin[...] = jnp.transpose(grad_in.astype(BF)).reshape(seq_count, block_len, width)
    if fused:
        second_z(G_OUT)
    gin_copies = exchange(rows_gin, gin_ref, 3, g_send, g_recv)
    if fused:
        second_link(G_IN)
        core_add(G_QKV)
        vector_step(0)
        first_link(G_O)
        first_z(G_IN)
        first_link(G_QKV)
        last_sum(G_OUT)
        vector_step(1)
        second_z(G_IN)
        second_link(G_QKV)
        second_link(G_O)
        vector_step(2)
        first_z(G_QKV)
        first_z(G_O)
        last_sum(G_IN)
        vector_step(3)
        second_z(G_QKV)
        second_z(G_O)
        finish(flight["p"])
        for k in range(seq_count):
            pooled_ref[k : k + 1, :] = pool_in[k, 0:1, :]
        vector_step(4)
        last_sum(G_QKV)
        last_sum(G_O)
    else:
        put(G_QKV)
        vecs_ref[...] = jnp.transpose(vec_cols[...])[0:16, :]
        pooled_ref[...] = jnp.transpose(vec_cols[...])[12:16, :]
    finish(out_copies)
    finish(gin_copies)


def deliver_kernel(*refs):
    out_in, gin_in, pooled_in, vecs_in = refs[:4]
    grads_in = refs[4:8]
    out_ref, gin_ref, pooled_ref = refs[8:11]
    grad_refs, vec_refs = refs[11:15], refs[15:24]
    grad_refs[0][...] = jnp.transpose(grads_in[0][...])
    moves = [(out_in, out_ref), (gin_in, gin_ref), (pooled_in, pooled_ref)]
    for src, dst in moves + list(zip(grads_in[1:], grad_refs[1:])):
        dst[...] = src[...]
    width = vecs_in.shape[1]
    for row, ref in zip((10, 11, 9, 7, 8, 3, 2, 0, 1), vec_refs):
        for i in range(ref.shape[0] // width):
            ref[i * width : (i + 1) * width] = vecs_in[row + i : row + i + 1, :].reshape(width)


def deliver(outs):
    out_hidden, grad_in, pooled, total, g_out, g_in, g_o, g_qkv = outs
    ff = total.shape[1] * g_out.shape[0] // g_qkv.shape[0]
    vmem = pl.BlockSpec(memory_space=pltpu.VMEM)
    arrays = (out_hidden, grad_in, pooled, g_out, g_in, g_o, g_qkv)
    lengths = [total.shape[1]] * 5 + [ff] + [total.shape[1]] * 3
    vectors = tuple(jax.ShapeDtypeStruct((n,), F32) for n in lengths)
    shapes = [jax.ShapeDtypeStruct(a.shape, a.dtype) for a in arrays]
    shapes[3] = jax.ShapeDtypeStruct(g_out.shape[::-1], F32)
    results = pl.pallas_call(
        deliver_kernel,
        out_shape=tuple(shapes) + vectors,
        in_specs=[vmem] * 8,
        out_specs=(vmem,) * 16,
        name="deliver",
    )(*outs)
    out_hidden, grad_in, pooled, g_out, g_in, g_o, g_qkv = results[:7]
    b_q, b_v, b_o, gain_one, shift_one, b_in, b_out, gain_two, shift_two = results[7:]
    return (
        out_hidden,
        pooled,
        grad_in,
        g_qkv,
        b_q,
        b_v,
        g_o,
        b_o,
        gain_one,
        shift_one,
        g_in,
        b_in,
        g_out.T,
        b_out,
        gain_two,
        shift_two,
    )


def body(
    hidden_in,
    lengths,
    w_qkv,
    b_q,
    b_v,
    w_o,
    b_o,
    gain_one,
    shift_one,
    w_in,
    b_in,
    w_out,
    b_out,
    gain_two,
    shift_two,
    cot_hidden,
    cot_pooled,
):
    batch_count, seq_count = lax.axis_size("batch"), lax.axis_size("seq")
    seqs_here, block_len, width = hidden_in.shape
    ff = w_in.shape[1]
    seq_len = seq_count * block_len
    assert seqs_here == seq_count
    fused = batch_count == 8 and seq_count == 4

    anywhere = pl.BlockSpec(memory_space=pl.ANY)
    vmem = pl.BlockSpec(memory_space=pltpu.VMEM)
    smem = pl.BlockSpec(memory_space=pltpu.SMEM)
    rows = jax.ShapeDtypeStruct(hidden_in.shape, BF)
    weights = (w_out, w_in, w_o, w_qkv)
    if fused:
        grads = tuple(
            jax.ShapeDtypeStruct((w.shape[0] // batch_count, w.shape[1] // seq_count), F32)
            for w in weights
        )
    else:
        grads = tuple(jax.ShapeDtypeStruct(w.shape, BF) for w in weights)
    dma = pltpu.SemaphoreType.DMA
    scratch = [pltpu.VMEM(w.shape, BF) for w in (w_qkv, w_o, w_in, w_out)]
    scratch += [
        pltpu.VMEM((seq_count, block_len, width), BF),
        pltpu.VMEM((seq_count, block_len, width), BF),
        pltpu.VMEM((width, seq_len), BF),
        pltpu.VMEM((3 * width, seq_len), BF),
        pltpu.VMEM((H * seq_len, seq_len), BF),
        pltpu.VMEM((H * 8, seq_len), F32),
        pltpu.VMEM((width, seq_len), BF),
        pltpu.VMEM((width, seq_len), F32),
        pltpu.VMEM((width, seq_len), BF),
        pltpu.VMEM((ff, seq_len), BF),
        pltpu.VMEM((ff, seq_len), BF),
        pltpu.VMEM((width, seq_len), F32),
        pltpu.VMEM((width, seq_len), BF),
        pltpu.VMEM((width, seq_len), BF),
        pltpu.VMEM((width, 128), F32),
        dma((4,)),
        dma((4,)),
    ]
    scratch += [dma((seq_count,))] * 8
    if fused:
        deep = width // batch_count
        blocks = (
            (ff // batch_count, width // 2),
            (deep * (ff // width), width // 2),
            (deep, width // 2),
            (deep * 3, width // 2),
        )
        z_blocks = tuple(
            (block[0] // 2, block[1]) if m == G_IN else (block[0] * block[1] // 256, 128)
            for m, block in enumerate(blocks)
        )
        scratch += [pltpu.VMEM((2, 2, 2) + blocks[0], BF)]
        scratch += [pltpu.VMEM((2, 2, 2) + block, BF) for block in blocks]
        scratch += [pltpu.VMEM((2, 2) + block, BF) for block in blocks]
        scratch += [pltpu.VMEM((2,) + block, BF) for block in blocks]
        scratch += [pltpu.VMEM((2, 2) + block, BF) for block in z_blocks]
        scratch += [pltpu.VMEM((2,) + block, BF) for block in z_blocks]
        scratch += [pltpu.VMEM(block, BF) for block in z_blocks]
        scratch += [dma((4, 4)), dma((4, 4)), dma((4, 8)), dma((4, 8))]
        scratch += [
            pltpu.VMEM((5, 16, width), F32),
            pltpu.VMEM((5, 16, width), F32),
            pltpu.VMEM((8, width), F32),
            pltpu.VMEM((seq_count, 8, width), F32),
            dma((5,)),
            dma((5,)),
            dma((seq_count,)),
            dma((seq_count,)),
        ]
    else:
        scratch += [pltpu.VMEM((width, ff), BF), dma((1,))]
    outs = pl.pallas_call(
        functools.partial(
            layer_kernel, (batch_count, seq_count, block_len, width, ff, fused)
        ),
        out_shape=(
            rows,
            rows,
            jax.ShapeDtypeStruct((seq_count, width), F32),
            jax.ShapeDtypeStruct((16, width), F32),
        )
        + grads,
        in_specs=[anywhere, anywhere, smem] + [vmem] * 10 + [anywhere] * 4,
        out_specs=(anywhere, anywhere, vmem, vmem) + (vmem if fused else anywhere,) * 4,
        scratch_shapes=scratch,
        compiler_params=pltpu.CompilerParams(
            collective_id=0, has_side_effects=True, vmem_limit_bytes=63 * 2**20
        ),
        name="encoder_layer",
    )(
        hidden_in,
        cot_hidden,
        lengths,
        cot_pooled,
        b_q,
        b_v,
        b_o,
        gain_one,
        shift_one,
        b_out,
        gain_two,
        shift_two,
        b_in,
        w_qkv,
        w_o,
        w_in,
        w_out,
    )
    if fused:
        return deliver(outs)
    out_hidden, grad_in, pooled, total, g_out, g_in, g_o, g_qkv = outs
    pooled = lax.all_gather(pooled[0], "seq", axis=0)
    total = lax.psum(total[:12], ("batch", "seq"))

    def scatter(grad):
        part = lax.psum_scatter(grad.astype(F32), "batch", scatter_dimension=0, tiled=True)
        part = lax.psum_scatter(part.astype(BF), "seq", scatter_dimension=1, tiled=True)
        return part.astype(F32)

    g_out, g_in, g_o, g_qkv = (scatter(g) for g in (g_out, g_in, g_o, g_qkv))
    return (
        out_hidden,
        pooled,
        grad_in,
        g_qkv,
        total[10],
        total[11],
        g_o,
        total[9],
        total[7],
        total[8],
        g_in,
        total[3:7].reshape(ff),
        g_out,
        total[2],
        total[0],
        total[1],
    )


def solution(mesh):
    rows = P("batch", "seq", None)
    shard = P("batch", "seq")
    in_specs = (rows, P("batch")) + (P(),) * 13 + (rows, P("batch", None))
    out_specs = (
        rows,
        P("batch", None),
        rows,
        shard,
        P(),
        P(),
        shard,
        P(),
        P(),
        P(),
        shard,
        P(),
        shard,
        P(),
        P(),
        P(),
    )
    return jax.shard_map(body, mesh=mesh, in_specs=in_specs, out_specs=out_specs, check_vma=False)
```

```python
import functools

import jax
import jax.numpy as jnp
from jax import lax
from jax.experimental import pallas as pl
from jax.experimental.pallas import tpu as pltpu
from jax.sharding import PartitionSpec as P

H = 12
BF = jnp.bfloat16
F32 = jnp.float32
MESH = pl.DeviceIdType.MESH
V_BQ, V_BV, V_BO, V_G1, V_S1, V_BOUT, V_G2, V_S2, V_CP, V_BIN = range(10)


def nn(a, b):
    return lax.dot_general(a, b, (((1,), (0,)), ((), ())), preferred_element_type=F32)


def nt(a, b):
    return lax.dot_general(a, b, (((1,), (1,)), ((), ())), preferred_element_type=F32)


def tn(a, b):
    return lax.dot_general(a, b, (((0,), (0,)), ((), ())), preferred_element_type=F32)


def aligned(index, size):
    return pl.ds(pl.multiple_of(index * size, size), size)


def norm_back(grad, normed, inv_std):
    first = jnp.mean(grad, 0, keepdims=True)
    second = jnp.mean(grad * normed, 0, keepdims=True)
    return inv_std * (grad - first - normed * second)


def add_low(a, b):
    return (a.astype(F32) + b.astype(F32)).astype(BF)


G_OUT, G_IN, G_O, G_QKV = range(4)


def layer_kernel(dims, *refs):
    batch_count, seq_count, block_len, width, ff, fused = dims
    refs = list(refs)

    def take(count):
        taken = refs[:count]
        del refs[:count]
        return taken

    hidden_ref, cot_ref, len_ref, cot_pool_ref = take(4)
    vectors = take(9)
    w_qkv_hbm, w_o_hbm, w_in_hbm, w_out_hbm = take(4)
    out_ref, gin_ref, pooled_ref, vecs_ref = take(4)
    grad_refs = take(4)
    w_qkv, w_o, w_in, w_out = take(4)
    x_rows, cot_rows, x_t, qkv_t, expo, inv_sum, att_t = take(7)
    normed_one, middle_low, act, slope, normed_two, low_a, grad_att = take(7)
    vec_cols, w_sem, own_sem = take(3)
    x_send, x_recv, c_send, c_recv, o_send, o_recv, g_send, g_recv = take(8)
    if fused:
        (send_core,) = take(1)
        held_core, held_one, held_two, held_z, z_one, z_two = (take(4) for _ in range(6))
        core_send, core_recv, link_send, link_recv = take(4)
        vec_own, vec_in, pool_own, pool_in, v_send, v_recv, p_send, p_recv = take(8)
    else:
        stage, put_sem = take(2)
    seq_len = seq_count * block_len
    head = width // H
    parts = ff // width
    me_b = lax.axis_index("batch")
    me_s = lax.axis_index("seq")

    loads = []
    for k, (src, dst) in enumerate(
        ((w_qkv_hbm, w_qkv), (w_o_hbm, w_o), (w_in_hbm, w_in), (w_out_hbm, w_out))
    ):
        load = pltpu.make_async_copy(src, dst, w_sem.at[k])
        load.start()
        loads.append(load)

    def flipped(index, bit):
        return index + bit - 2 * bit * lax.rem(index // bit, 2)

    def seq_peer(d):
        return (me_b, lax.rem(me_s + d, seq_count))

    core, at_x, at_y = lax.rem(me_b, 2), lax.rem(me_b // 2, 2), lax.rem(me_b // 4, 2)
    z_lo, z_hi = lax.rem(me_s, 2), lax.rem(me_s // 2, 2)
    to_core, to_x, to_y = ((flipped(me_b, bit), me_s) for bit in (1, 2, 4))
    to_z_lo, to_z_hi = ((me_b, flipped(me_s, bit)) for bit in (1, 2))

    barrier = pltpu.get_barrier_semaphore()
    greeted = [seq_peer(d) for d in range(1, seq_count)]
    if fused:
        greeted += [to_core, to_x, to_y]
    for device in greeted:
        pl.semaphore_signal(barrier, inc=1, device_id=device, device_id_type=MESH)
    pl.semaphore_wait(barrier, len(greeted))

    def remote(src, dst, device, send_sem, recv_sem):
        copy = pltpu.make_async_remote_copy(
            src_ref=src,
            dst_ref=dst,
            send_sem=send_sem,
            recv_sem=recv_sem,
            device_id=device,
            device_id_type=MESH,
        )
        copy.start()
        return copy

    def exchange(src, dst, own, send_sem, recv_sem):
        copies = []
        for d in range(1, seq_count):
            to = lax.rem(me_s + d, seq_count)
            copies.append(
                remote(src.at[to], dst.at[me_s], seq_peer(d), send_sem.at[d], recv_sem.at[d])
            )
        copy = pltpu.make_async_copy(src.at[me_s], dst.at[me_s], own_sem.at[own])
        copy.start()
        copies.append(copy)
        return copies

    def finish(copies):
        for copy in copies:
            copy.wait()

    hidden_copies = exchange(hidden_ref, x_rows, 0, x_send, x_recv)

    cot_pool = cot_pool_ref[...].astype(F32)
    is_mine = lax.broadcasted_iota(jnp.int32, cot_pool.shape, 0) == me_s
    cot_pool = jnp.sum(jnp.where(is_mine, cot_pool, 0.0), 0, keepdims=True)
    rows = [ref[...].astype(F32).reshape(1, width) for ref in vectors[:8]] + [cot_pool]
    for i in range(parts):
        rows.append(vectors[8][i * width : (i + 1) * width].astype(F32).reshape(1, width))
    rows.append(jnp.zeros((128 - len(rows), width), F32))
    vec_t = jnp.transpose(jnp.concatenate(rows, 0))
    vec_cols[...] = jnp.zeros((width, 128), F32)

    def column(index):
        return vec_t[:, index : index + 1]

    length = len_ref[me_s]
    inv_len = 1.0 / jnp.full((1, seq_len), length, jnp.int32).astype(F32)
    token_at = lax.broadcasted_iota(jnp.int32, (1, seq_len), 1)
    live = jnp.where(token_at < length, 1.0, 0.0).astype(F32)
    key_at = lax.broadcasted_iota(jnp.int32, (seq_len, 1), 0)
    key_bias = jnp.where(key_at < length, 0.0, -1e30).astype(F32)

    finish(hidden_copies)
    cot_copies = exchange(cot_ref, cot_rows, 1, c_send, c_recv)
    x_t[...] = jnp.transpose(x_rows[...].reshape(seq_len, width))

    loads[0].wait()
    scale = head ** (-0.5)
    qkv_t[0:width, :] = (
        (tn(w_qkv[:, 0:width], x_t[...]) + column(V_BQ)) * scale
    ).astype(BF)
    qkv_t[width : 2 * width, :] = tn(w_qkv[:, width : 2 * width], x_t[...]).astype(BF)
    qkv_t[2 * width :, :] = (tn(w_qkv[:, 2 * width :], x_t[...]) + column(V_BV)).astype(BF)

    def head_rows(h, third):
        return pl.ds(pl.multiple_of(h * head + third * width, head), head)

    def attend(h, carry):
        scores = tn(qkv_t[head_rows(h, 1), :], qkv_t[head_rows(h, 0), :]) + key_bias
        top = jnp.max(scores, 0, keepdims=True)
        weights = jnp.exp(scores - top)
        inverse = 1.0 / jnp.sum(weights, 0, keepdims=True)
        weights_low = weights.astype(BF)
        expo[aligned(h, seq_len), :] = weights_low
        inv_sum[aligned(h, 8), :] = jnp.broadcast_to(inverse, (8, seq_len))
        att_t[head_rows(h, 0), :] = (nn(qkv_t[head_rows(h, 2), :], weights_low) * inverse).astype(BF)
        return carry

    lax.fori_loop(0, H, attend, 0, unroll=4)

    loads[1].wait()
    summed = x_t[...].astype(F32) + (tn(w_o[...], att_t[...]) + column(V_BO))
    centred = summed - jnp.mean(summed, 0, keepdims=True)
    inv_one = lax.rsqrt(jnp.mean(centred * centred, 0, keepdims=True) + 1e-12)
    normed_one[...] = centred * inv_one
    middle_low[...] = (normed_one[...] * column(V_G1) + column(V_S1)).astype(BF)

    loads[2].wait()
    for i in range(parts):
        rows = slice(i * width, (i + 1) * width)
        pre = tn(w_in[:, rows], middle_low[...]) + column(V_BIN + i)
        cumulative = 0.5 * (1.0 + lax.erf(pre * 0.7071067811865476))
        density = jnp.exp(-0.5 * pre * pre) * 0.3989422804014327
        act[rows, :] = (pre * cumulative).astype(BF)
        slope[rows, :] = (cumulative + pre * density).astype(BF)
    loads[3].wait()
    middle = normed_one[...] * column(V_G1) + column(V_S1)
    summed = middle + (tn(w_out[...], act[...]) + column(V_BOUT))
    centred = summed - jnp.mean(summed, 0, keepdims=True)
    inv_two = lax.rsqrt(jnp.mean(centred * centred, 0, keepdims=True) + 1e-12)
    normed_two[...] = centred * inv_two
    finish(cot_copies)
    grad_final = jnp.transpose(cot_rows[...].reshape(seq_len, width)).astype(F32)
    grad_final = grad_final + column(V_CP) * (live * inv_len)
    low_a[...] = norm_back(grad_final * column(V_G2), normed_two[...], inv_two).astype(BF)

    def whole_grad(m):
        if m == G_OUT:
            rows, columns = act, low_a
        elif m == G_IN:
            rows, columns = middle_low, slope
        elif m == G_O:
            rows, columns = att_t, low_a
        else:
            rows, columns = x_t, qkv_t
        return rows, columns

    def put(m):
        rows, columns = whole_grad(m)
        for i in range(rows.shape[0] // width):
            value = nt(rows[i * width : (i + 1) * width, :], columns[...])
            here = stage.at[:, 0 : value.shape[1]]
            here[...] = value.astype(BF)
            copy = pltpu.make_async_copy(
                here, grad_refs[m].at[i * width : (i + 1) * width, :], put_sem.at[0]
            )
            copy.start()
            copy.wait()

    flight = {}

    def partial(m, which):
        rows, columns = whole_grad(m)
        deep = rows.shape[0] // batch_count
        left = jnp.concatenate([rows[aligned(2 * j + which, deep), :] for j in range(4)], 0)
        tile = width // 2
        half = columns.shape[0] // 2
        for h in range(2):
            value = nt(left, columns[h * half : (h + 1) * half, :])
            for j in range(4):
                for t in range(half // tile):
                    block = value[j * deep : (j + 1) * deep, t * tile : (t + 1) * tile]
                    yield h, j, slice(t * deep, (t + 1) * deep), block

    def core_buffer(m):
        rows = held_core[m].shape[3]
        start = held_core[G_O].shape[3] if m == G_QKV else 0
        return send_core.at[:, :, :, start : start + rows, :]

    def core_start(m):
        buffer = core_buffer(m)
        if m == G_IN:
            for copy in flight[G_OUT, 0]:
                copy.wait_send()
        if m == G_O:
            for copy in flight[G_IN, 0]:
                copy.wait_send()
        for h, j, rows, block in partial(m, 1 - core):
            buffer[h, j // 2, j % 2, rows, :] = block.astype(BF)
        flight[m, 0] = [
            remote(buffer, held_core[m], to_core, core_send.at[m, 0], core_recv.at[m, 0])
        ]

    def core_add(m):
        for copy in flight[m, 0]:
            copy.wait_recv()
            if m in (G_O, G_QKV):
                copy.wait_send()
        held = held_core[m]
        for h, j, rows, block in partial(m, core):
            held[h, j // 2, j % 2, rows, :] = add_low(held[h, j // 2, j % 2, rows, :], block)

    def first_link(m):
        held = held_core[m]
        flight[m, 1] = [
            remote(
                held.at[0, :, 1 - at_x],
                held_one[m].at[0],
                to_x,
                link_send.at[m, 0],
                link_recv.at[m, 0],
            ),
            remote(
                held.at[1, 1 - at_y],
                held_one[m].at[1],
                to_y,
                link_send.at[m, 1],
                link_recv.at[m, 1],
            ),
        ]

    order = ((1 - at_y, 1 - at_x), (at_y, 1 - at_x), (1 - at_y, at_x), (at_y, at_x))

    def first_block(y, x, which):
        deep = ff // batch_count
        row = aligned(4 * y + 2 * x + which, deep)
        return nt(act[row, :], low_a[...])

    def first_send(k):
        y, x = order[k]
        value = first_block(y, x, 1 - core)
        half = value.shape[1] // 2
        send_core[0, y, x] = value[:, :half].astype(BF)
        send_core[1, y, x] = value[:, half:].astype(BF)
        flight[G_OUT, 0].append(
            remote(
                send_core.at[:, y, x],
                held_core[G_OUT].at[:, y, x],
                to_core,
                core_send.at[G_OUT, k],
                core_recv.at[G_OUT, k],
            )
        )

    def first_add(k):
        held, after = held_core[G_OUT], held_one[G_OUT]
        y, x = order[k]
        value = first_block(y, x, core)
        half = value.shape[1] // 2
        flight[G_OUT, 0][k].wait_recv()
        held[0, y, x] = add_low(held[0, y, x], value[:, :half])
        held[1, y, x] = add_low(held[1, y, x], value[:, half:])
        hops = []
        if k in (0, 1):
            hops.append((0, after.at[0, y], to_x, k))
        if k in (0, 2):
            hops.append((1, after.at[1, x], to_y, 2 + k // 2))
        for h, dst, device, sem in hops:
            flight[G_OUT, 1].append(
                remote(
                    held.at[h, y, x],
                    dst,
                    device,
                    link_send.at[G_OUT, sem],
                    link_recv.at[G_OUT, sem],
                )
            )

    def first_sums():
        flight[G_OUT, 0], flight[G_OUT, 1] = [], []
        first_send(0)
        first_send(1)
        first_add(0)
        first_send(2)
        first_send(3)
        for k in range(1, 4):
            first_add(k)

    def second_link(m):
        finish(flight[m, 1])
        held, after = held_core[m], held_one[m]
        after[0, 1 - at_y] = add_low(after[0, 1 - at_y], held[0, 1 - at_y, at_x])
        after[1, 1 - at_x] = add_low(after[1, 1 - at_x], held[1, at_y, 1 - at_x])
        flight[m, 2] = [
            remote(
                after.at[0, 1 - at_y],
                held_two[m].at[0],
                to_y,
                link_send.at[m, 4],
                link_recv.at[m, 4],
            ),
            remote(
                after.at[1, 1 - at_x],
                held_two[m].at[1],
                to_x,
                link_send.at[m, 5],
                link_recv.at[m, 5],
            ),
        ]
        after[0, at_y] = add_low(after[0, at_y], held[0, at_y, at_x])
        after[1, at_x] = add_low(after[1, at_x], held[1, at_y, at_x])

    def first_z(m):
        finish(flight[m, 2])
        after, last, ready = held_one[m], held_two[m], held_z[m]
        for h in range(2):
            mine = after[0, at_y] if h == 0 else after[1, at_x]
            block = last[h].astype(F32) + mine.astype(F32)
            if m == G_IN:
                deep = block.shape[0] // 2
                for k in range(2):
                    ready[h, k] = block[k * deep : (k + 1) * deep, :].astype(BF)
                continue
            deep = grad_refs[m].shape[0]
            per_row = width // 256
            count = block.shape[0] // deep * per_row
            tiles = []
            for t in range(count):
                row, lane = t // per_row * deep, t % per_row * 128
                tiles.append(block[row : row + deep, lane : lane + 128])
            full = count // 2
            for k in range(2):
                for t in range(full):
                    ready[h, k, t * deep : (t + 1) * deep, :] = tiles[t + k * (full + 1)].astype(BF)
            turned = pltpu.roll(tiles[full], 64, 1)
            left = lax.broadcasted_iota(jnp.int32, (deep // 2, 128), 1) < 64
            upper, lower = slice(0, deep // 2), slice(deep // 2, deep)
            folded = (
                jnp.where(left, tiles[full][upper], turned[lower]),
                jnp.where(left, turned[upper], tiles[full][lower]),
            )
            for k in range(2):
                ready[h, k, full * deep :, :] = folded[k].astype(BF)
        flight[m, 3] = [
            remote(
                ready.at[:, 1 - z_lo], z_one[m], to_z_lo, link_send.at[m, 6], link_recv.at[m, 6]
            )
        ]

    def second_z(m):
        finish(flight[m, 3])
        z_one[m][1 - z_hi] = add_low(z_one[m][1 - z_hi], held_z[m][1 - z_hi, z_lo])
        flight[m, 4] = [
            remote(
                z_one[m].at[1 - z_hi], z_two[m], to_z_hi, link_send.at[m, 7], link_recv.at[m, 7]
            )
        ]

    def last_sum(m):
        mine = z_one[m][z_hi].astype(F32) + held_z[m][z_hi, z_lo].astype(F32)
        finish(flight[m, 4])
        total = mine + z_two[m][...].astype(F32)
        out = grad_refs[m]
        deep, wide = out.shape
        if m == G_IN:
            out[:, : wide // 2] = total[:deep, :]
            out[:, wide // 2 :] = total[deep:, :]
            return
        full = wide // 128
        tiles = [total[t * deep : (t + 1) * deep, :] for t in range(full)]
        folded = total[full * deep :, :]
        turned = pltpu.roll(folded, 64, 1)
        after_tiles = jnp.concatenate(tiles + [jnp.concatenate([folded, turned], 0)], 1)
        before_tiles = jnp.concatenate([jnp.concatenate([turned, folded], 0)] + tiles, 1)
        before_tiles = pltpu.roll(before_tiles, full * 128 + 64, 1)
        out[...] = jnp.where(z_lo == 0, after_tiles, before_tiles)[:, :wide]

    peers = (to_core, to_x, to_y, to_z_lo, to_z_hi)

    def vector_start():
        vec_own[0] = jnp.transpose(vec_cols[...])[0:16, :]
        flight["v"] = remote(vec_own.at[0], vec_in.at[0], peers[0], v_send.at[0], v_recv.at[0])

    def vector_step(k):
        flight["v"].wait()
        total = vec_own[k] + vec_in[k]
        if k == 4:
            vecs_ref[...] = total
        else:
            vec_own[k + 1] = total
            flight["v"] = remote(
                vec_own.at[k + 1],
                vec_in.at[k + 1],
                peers[k + 1],
                v_send.at[k + 1],
                v_recv.at[k + 1],
            )

    if fused:
        first_sums()
    else:
        put(G_OUT)

    rows_out = x_rows
    output = normed_two[...] * column(V_G2) + column(V_S2)
    rows_out[...] = jnp.transpose(output.astype(BF)).reshape(seq_count, block_len, width)
    out_copies = exchange(rows_out, out_ref, 2, o_send, o_recv)
    pooled_col = jnp.sum(output * (live * inv_len), 1, keepdims=True)
    if fused:
        pool_own[...] = jnp.transpose(jnp.broadcast_to(pooled_col, (width, 128)))[0:8, :]
        pool_in[me_s] = pool_own[...]
        flight["p"] = [
            remote(pool_own, pool_in.at[me_s], seq_peer(d), p_send.at[d], p_recv.at[d])
            for d in range(1, seq_count)
        ]
    else:
        vec_cols[:, 12:13] = pooled_col
    grad_final = jnp.transpose(cot_rows[...].reshape(seq_len, width)).astype(F32)
    grad_final = grad_final + column(V_CP) * (live * inv_len)
    vec_cols[:, 0:1] = jnp.sum(grad_final * normed_two[...], 1, keepdims=True)
    vec_cols[:, 1:2] = jnp.sum(grad_final, 1, keepdims=True)
    vec_cols[:, 2:3] = jnp.sum(low_a[...].astype(F32), 1, keepdims=True)

    for i in range(parts):
        rows = slice(i * width, (i + 1) * width)
        grad_act_low = nn(w_out[rows, :], low_a[...]).astype(BF)
        grad_pre = (grad_act_low.astype(F32) * slope[rows, :].astype(F32)).astype(BF)
        slope[rows, :] = grad_pre
        vec_cols[:, 3 + i : 4 + i] = jnp.sum(grad_pre.astype(F32), 1, keepdims=True)
    if fused:
        core_start(G_IN)
    else:
        put(G_IN)
    grad_middle = low_a[...].astype(F32) + nn(w_in[...], slope[...])
    if fused:
        second_link(G_OUT)

    vec_cols[:, 7:8] = jnp.sum(grad_middle * normed_one[...], 1, keepdims=True)
    vec_cols[:, 8:9] = jnp.sum(grad_middle, 1, keepdims=True)
    grad_first = normed_two
    grad_first[...] = norm_back(grad_middle * column(V_G1), normed_one[...], inv_one)
    low_a[...] = grad_first[...].astype(BF)
    vec_cols[:, 9:10] = jnp.sum(low_a[...].astype(F32), 1, keepdims=True)
    if fused:
        core_add(G_IN)
        first_link(G_IN)
        core_start(G_O)
    else:
        put(G_O)
    grad_heads = nn(w_o[...], low_a[...])
    for h in range(H):
        rows = slice(h * head, (h + 1) * head)
        grad_att[rows, :] = (grad_heads[rows, :] * inv_sum[h * 8 : h * 8 + 1, :]).astype(BF)
    if fused:
        core_add(G_O)

    def attend_back(h, carry):
        grad = grad_att[head_rows(h, 0), :]
        inner = jnp.sum(grad.astype(F32) * att_t[head_rows(h, 0), :].astype(F32), 0, keepdims=True)
        weights_low = expo[aligned(h, seq_len), :]
        queries, keys, values = (qkv_t[head_rows(h, third), :] for third in range(3))
        grad_probs = tn(values, grad)
        grad_scores = (weights_low.astype(F32) * (grad_probs - inner)).astype(BF)
        qkv_t[head_rows(h, 0), :] = (nn(keys, grad_scores) * scale).astype(BF)
        qkv_t[head_rows(h, 1), :] = nt(queries, grad_scores).astype(BF)
        qkv_t[head_rows(h, 2), :] = nt(grad, weights_low).astype(BF)
        return carry

    if fused:
        for k in range(3):
            lax.fori_loop(k * (H // 3), (k + 1) * (H // 3), attend_back, 0)
            if k == 0:
                first_z(G_OUT)
    else:
        lax.fori_loop(0, H, attend_back, 0)
    vec_cols[:, 10:11] = jnp.sum(qkv_t[0:width, :].astype(F32), 1, keepdims=True)
    vec_cols[:, 11:12] = jnp.sum(qkv_t[2 * width :, :].astype(F32), 1, keepdims=True)
    if fused:
        vector_start()
        core_start(G_QKV)
    grad_in = nn(w_qkv[...], qkv_t[...]) + grad_first[...]
    rows_gin = cot_rows
    rows_gin[...] = jnp.transpose(grad_in.astype(BF)).reshape(seq_count, block_len, width)
    if fused:
        second_z(G_OUT)
    gin_copies = exchange(rows_gin, gin_ref, 3, g_send, g_recv)
    if fused:
        second_link(G_IN)
        core_add(G_QKV)
        vector_step(0)
        first_link(G_O)
        first_z(G_IN)
        first_link(G_QKV)
        last_sum(G_OUT)
        vector_step(1)
        second_z(G_IN)
        second_link(G_QKV)
        second_link(G_O)
        vector_step(2)
        first_z(G_QKV)
        first_z(G_O)
        last_sum(G_IN)
        vector_step(3)
        second_z(G_QKV)
        second_z(G_O)
        finish(flight["p"])
        for k in range(seq_count):
            pooled_ref[k : k + 1, :] = pool_in[k, 0:1, :]
        vector_step(4)
        last_sum(G_QKV)
        last_sum(G_O)
    else:
        put(G_QKV)
        vecs_ref[...] = jnp.transpose(vec_cols[...])[0:16, :]
        pooled_ref[...] = jnp.transpose(vec_cols[...])[12:16, :]
    finish(out_copies)
    finish(gin_copies)


def deliver_kernel(*refs):
    out_in, gin_in, pooled_in, vecs_in = refs[:4]
    grads_in = refs[4:8]
    out_ref, gin_ref, pooled_ref = refs[8:11]
    grad_refs, vec_refs = refs[11:15], refs[15:24]
    grad_refs[0][...] = jnp.transpose(grads_in[0][...])
    moves = [(out_in, out_ref), (gin_in, gin_ref), (pooled_in, pooled_ref)]
    for src, dst in moves + list(zip(grads_in[1:], grad_refs[1:])):
        dst[...] = src[...]
    width = vecs_in.shape[1]
    for row, ref in zip((10, 11, 9, 7, 8, 3, 2, 0, 1), vec_refs):
        for i in range(ref.shape[0] // width):
            ref[i * width : (i + 1) * width] = vecs_in[row + i : row + i + 1, :].reshape(width)


def deliver(outs):
    out_hidden, grad_in, pooled, total, g_out, g_in, g_o, g_qkv = outs
    ff = total.shape[1] * g_out.shape[0] // g_qkv.shape[0]
    vmem = pl.BlockSpec(memory_space=pltpu.VMEM)
    arrays = (out_hidden, grad_in, pooled, g_out, g_in, g_o, g_qkv)
    lengths = [total.shape[1]] * 5 + [ff] + [total.shape[1]] * 3
    vectors = tuple(jax.ShapeDtypeStruct((n,), F32) for n in lengths)
    shapes = [jax.ShapeDtypeStruct(a.shape, a.dtype) for a in arrays]
    shapes[3] = jax.ShapeDtypeStruct(g_out.shape[::-1], F32)
    results = pl.pallas_call(
        deliver_kernel,
        out_shape=tuple(shapes) + vectors,
        in_specs=[vmem] * 8,
        out_specs=(vmem,) * 16,
        name="deliver",
    )(*outs)
    out_hidden, grad_in, pooled, g_out, g_in, g_o, g_qkv = results[:7]
    b_q, b_v, b_o, gain_one, shift_one, b_in, b_out, gain_two, shift_two = results[7:]
    return (
        out_hidden,
        pooled,
        grad_in,
        g_qkv,
        b_q,
        b_v,
        g_o,
        b_o,
        gain_one,
        shift_one,
        g_in,
        b_in,
        g_out.T,
        b_out,
        gain_two,
        shift_two,
    )


def body(
    hidden_in,
    lengths,
    w_qkv,
    b_q,
    b_v,
    w_o,
    b_o,
    gain_one,
    shift_one,
    w_in,
    b_in,
    w_out,
    b_out,
    gain_two,
    shift_two,
    cot_hidden,
    cot_pooled,
):
    batch_count, seq_count = lax.axis_size("batch"), lax.axis_size("seq")
    seqs_here, block_len, width = hidden_in.shape
    ff = w_in.shape[1]
    seq_len = seq_count * block_len
    assert seqs_here == seq_count
    fused = batch_count == 8 and seq_count == 4

    anywhere = pl.BlockSpec(memory_space=pl.ANY)
    vmem = pl.BlockSpec(memory_space=pltpu.VMEM)
    smem = pl.BlockSpec(memory_space=pltpu.SMEM)
    rows = jax.ShapeDtypeStruct(hidden_in.shape, BF)
    weights = (w_out, w_in, w_o, w_qkv)
    if fused:
        grads = tuple(
            jax.ShapeDtypeStruct((w.shape[0] // batch_count, w.shape[1] // seq_count), F32)
            for w in weights
        )
    else:
        grads = tuple(jax.ShapeDtypeStruct(w.shape, BF) for w in weights)
    dma = pltpu.SemaphoreType.DMA
    scratch = [pltpu.VMEM(w.shape, BF) for w in (w_qkv, w_o, w_in, w_out)]
    scratch += [
        pltpu.VMEM((seq_count, block_len, width), BF),
        pltpu.VMEM((seq_count, block_len, width), BF),
        pltpu.VMEM((width, seq_len), BF),
        pltpu.VMEM((3 * width, seq_len), BF),
        pltpu.VMEM((H * seq_len, seq_len), BF),
        pltpu.VMEM((H * 8, seq_len), F32),
        pltpu.VMEM((width, seq_len), BF),
        pltpu.VMEM((width, seq_len), F32),
        pltpu.VMEM((width, seq_len), BF),
        pltpu.VMEM((ff, seq_len), BF),
        pltpu.VMEM((ff, seq_len), BF),
        pltpu.VMEM((width, seq_len), F32),
        pltpu.VMEM((width, seq_len), BF),
        pltpu.VMEM((width, seq_len), BF),
        pltpu.VMEM((width, 128), F32),
        dma((4,)),
        dma((4,)),
    ]
    scratch += [dma((seq_count,))] * 8
    if fused:
        deep = width // batch_count
        blocks = (
            (ff // batch_count, width // 2),
            (deep * (ff // width), width // 2),
            (deep, width // 2),
            (deep * 3, width // 2),
        )
        z_blocks = tuple(
            (block[0] // 2, block[1]) if m == G_IN else (block[0] * block[1] // 256, 128)
            for m, block in enumerate(blocks)
        )
        scratch += [pltpu.VMEM((2, 2, 2) + blocks[0], BF)]
        scratch += [pltpu.VMEM((2, 2, 2) + block, BF) for block in blocks]
        scratch += [pltpu.VMEM((2, 2) + block, BF) for block in blocks]
        scratch += [pltpu.VMEM((2,) + block, BF) for block in blocks]
        scratch += [pltpu.VMEM((2, 2) + block, BF) for block in z_blocks]
        scratch += [pltpu.VMEM((2,) + block, BF) for block in z_blocks]
        scratch += [pltpu.VMEM(block, BF) for block in z_blocks]
        scratch += [dma((4, 4)), dma((4, 4)), dma((4, 8)), dma((4, 8))]
        scratch += [
            pltpu.VMEM((5, 16, width), F32),
            pltpu.VMEM((5, 16, width), F32),
            pltpu.VMEM((8, width), F32),
            pltpu.VMEM((seq_count, 8, width), F32),
            dma((5,)),
            dma((5,)),
            dma((seq_count,)),
            dma((seq_count,)),
        ]
    else:
        scratch += [pltpu.VMEM((width, ff), BF), dma((1,))]
    outs = pl.pallas_call(
        functools.partial(
            layer_kernel, (batch_count, seq_count, block_len, width, ff, fused)
        ),
        out_shape=(
            rows,
            rows,
            jax.ShapeDtypeStruct((seq_count, width), F32),
            jax.ShapeDtypeStruct((16, width), F32),
        )
        + grads,
        in_specs=[anywhere, anywhere, smem] + [vmem] * 10 + [anywhere] * 4,
        out_specs=(anywhere, anywhere, vmem, vmem) + (vmem if fused else anywhere,) * 4,
        scratch_shapes=scratch,
        compiler_params=pltpu.CompilerParams(
            collective_id=0, has_side_effects=True, vmem_limit_bytes=63 * 2**20
        ),
        name="encoder_layer",
    )(
        hidden_in,
        cot_hidden,
        lengths,
        cot_pooled,
        b_q,
        b_v,
        b_o,
        gain_one,
        shift_one,
        b_out,
        gain_two,
        shift_two,
        b_in,
        w_qkv,
        w_o,
        w_in,
        w_out,
    )
    if fused:
        return deliver(outs)
    out_hidden, grad_in, pooled, total, g_out, g_in, g_o, g_qkv = outs
    pooled = lax.all_gather(pooled[0], "seq", axis=0)
    total = lax.psum(total[:12], ("batch", "seq"))

    def scatter(grad):
        part = lax.psum_scatter(grad.astype(F32), "batch", scatter_dimension=0, tiled=True)
        part = lax.psum_scatter(part.astype(BF), "seq", scatter_dimension=1, tiled=True)
        return part.astype(F32)

    g_out, g_in, g_o, g_qkv = (scatter(g) for g in (g_out, g_in, g_o, g_qkv))
    return (
        out_hidden,
        pooled,
        grad_in,
        g_qkv,
        total[10],
        total[11],
        g_o,
        total[9],
        total[7],
        total[8],
        g_in,
        total[3:7].reshape(ff),
        g_out,
        total[2],
        total[0],
        total[1],
    )


def solution(mesh):
    rows = P("batch", "seq", None)
    shard = P("batch", "seq")
    in_specs = (rows, P("batch")) + (P(),) * 13 + (rows, P("batch", None))
    out_specs = (
        rows,
        P("batch", None),
        rows,
        shard,
        P(),
        P(),
        shard,
        P(),
        P(),
        P(),
        shard,
        P(),
        shard,
        P(),
        P(),
        P(),
    )
    return jax.shard_map(body, mesh=mesh, in_specs=in_specs, out_specs=out_specs, check_vma=False)
```

```python
import functools

import jax
import jax.numpy as jnp
from jax import lax
from jax.experimental import pallas as pl
from jax.experimental.pallas import tpu as pltpu
from jax.sharding import PartitionSpec as P

H = 12
BF = jnp.bfloat16
F32 = jnp.float32
MESH = pl.DeviceIdType.MESH
V_BQ, V_BV, V_BO, V_G1, V_S1, V_BOUT, V_G2, V_S2, V_CP, V_BIN = range(10)


def nn(a, b):
    return lax.dot_general(a, b, (((1,), (0,)), ((), ())), preferred_element_type=F32)


def nt(a, b):
    return lax.dot_general(a, b, (((1,), (1,)), ((), ())), preferred_element_type=F32)


def tn(a, b):
    return lax.dot_general(a, b, (((0,), (0,)), ((), ())), preferred_element_type=F32)


def aligned(index, size):
    return pl.ds(pl.multiple_of(index * size, size), size)


def norm_back(grad, normed, inv_std):
    first = jnp.mean(grad, 0, keepdims=True)
    second = jnp.mean(grad * normed, 0, keepdims=True)
    return inv_std * (grad - first - normed * second)


def add_low(a, b):
    return (a.astype(F32) + b.astype(F32)).astype(BF)


G_OUT, G_IN, G_O, G_QKV = range(4)


def layer_kernel(dims, *refs):
    batch_count, seq_count, block_len, width, ff, fused = dims
    refs = list(refs)

    def take(count):
        taken = refs[:count]
        del refs[:count]
        return taken

    hidden_ref, cot_ref, len_ref, cot_pool_ref = take(4)
    vectors = take(9)
    w_qkv_hbm, w_o_hbm, w_in_hbm, w_out_hbm = take(4)
    out_ref, gin_ref, pooled_ref, vecs_ref = take(4)
    grad_refs = take(4)
    w_qkv, w_o, w_in, w_out = take(4)
    x_rows, cot_rows, x_t, qkv_t, expo, inv_sum, att_t = take(7)
    normed_one, middle_low, act, slope, normed_two, low_a, grad_att = take(7)
    vec_cols, w_sem, own_sem = take(3)
    x_send, x_recv, c_send, c_recv, o_send, o_recv, g_send, g_recv = take(8)
    if fused:
        (send_core,) = take(1)
        held_core, held_one, held_two, held_z, z_one, z_two = (take(4) for _ in range(6))
        core_send, core_recv, link_send, link_recv = take(4)
        vec_own, vec_in, pool_own, pool_in, v_send, v_recv, p_send, p_recv = take(8)
    else:
        stage, put_sem = take(2)
    seq_len = seq_count * block_len
    head = width // H
    parts = ff // width
    me_b = lax.axis_index("batch")
    me_s = lax.axis_index("seq")

    loads = []
    for k, (src, dst) in enumerate(
        ((w_qkv_hbm, w_qkv), (w_o_hbm, w_o), (w_in_hbm, w_in), (w_out_hbm, w_out))
    ):
        load = pltpu.make_async_copy(src, dst, w_sem.at[k])
        load.start()
        loads.append(load)

    def flipped(index, bit):
        return index + bit - 2 * bit * lax.rem(index // bit, 2)

    def seq_peer(d):
        return (me_b, lax.rem(me_s + d, seq_count))

    core, at_x, at_y = lax.rem(me_b, 2), lax.rem(me_b // 2, 2), lax.rem(me_b // 4, 2)
    z_lo, z_hi = lax.rem(me_s, 2), lax.rem(me_s // 2, 2)
    to_core, to_x, to_y = ((flipped(me_b, bit), me_s) for bit in (1, 2, 4))
    to_z_lo, to_z_hi = ((me_b, flipped(me_s, bit)) for bit in (1, 2))

    barrier = pltpu.get_barrier_semaphore()
    greeted = [seq_peer(d) for d in range(1, seq_count)]
    if fused:
        greeted += [to_core, to_x, to_y]
    for device in greeted:
        pl.semaphore_signal(barrier, inc=1, device_id=device, device_id_type=MESH)
    pl.semaphore_wait(barrier, len(greeted))

    def remote(src, dst, device, send_sem, recv_sem):
        copy = pltpu.make_async_remote_copy(
            src_ref=src,
            dst_ref=dst,
            send_sem=send_sem,
            recv_sem=recv_sem,
            device_id=device,
            device_id_type=MESH,
        )
        copy.start()
        return copy

    def exchange(src, dst, own, send_sem, recv_sem):
        copies = []
        for d in range(1, seq_count):
            to = lax.rem(me_s + d, seq_count)
            copies.append(
                remote(src.at[to], dst.at[me_s], seq_peer(d), send_sem.at[d], recv_sem.at[d])
            )
        copy = pltpu.make_async_copy(src.at[me_s], dst.at[me_s], own_sem.at[own])
        copy.start()
        copies.append(copy)
        return copies

    def finish(copies):
        for copy in copies:
            copy.wait()

    hidden_copies = exchange(hidden_ref, x_rows, 0, x_send, x_recv)

    cot_pool = cot_pool_ref[...].astype(F32)
    is_mine = lax.broadcasted_iota(jnp.int32, cot_pool.shape, 0) == me_s
    cot_pool = jnp.sum(jnp.where(is_mine, cot_pool, 0.0), 0, keepdims=True)
    rows = [ref[...].astype(F32).reshape(1, width) for ref in vectors[:8]] + [cot_pool]
    for i in range(parts):
        rows.append(vectors[8][i * width : (i + 1) * width].astype(F32).reshape(1, width))
    rows.append(jnp.zeros((128 - len(rows), width), F32))
    vec_t = jnp.transpose(jnp.concatenate(rows, 0))
    vec_cols[...] = jnp.zeros((width, 128), F32)

    def column(index):
        return vec_t[:, index : index + 1]

    length = len_ref[me_s]
    inv_len = 1.0 / jnp.full((1, seq_len), length, jnp.int32).astype(F32)
    token_at = lax.broadcasted_iota(jnp.int32, (1, seq_len), 1)
    live = jnp.where(token_at < length, 1.0, 0.0).astype(F32)
    key_at = lax.broadcasted_iota(jnp.int32, (seq_len, 1), 0)
    key_bias = jnp.where(key_at < length, 0.0, -1e30).astype(F32)

    finish(hidden_copies)
    cot_copies = exchange(cot_ref, cot_rows, 1, c_send, c_recv)
    x_t[...] = jnp.transpose(x_rows[...].reshape(seq_len, width))

    loads[0].wait()
    scale = head ** (-0.5)
    qkv_t[0:width, :] = (
        (tn(w_qkv[:, 0:width], x_t[...]) + column(V_BQ)) * scale
    ).astype(BF)
    qkv_t[width : 2 * width, :] = tn(w_qkv[:, width : 2 * width], x_t[...]).astype(BF)
    qkv_t[2 * width :, :] = (tn(w_qkv[:, 2 * width :], x_t[...]) + column(V_BV)).astype(BF)

    def head_rows(h, third):
        return pl.ds(pl.multiple_of(h * head + third * width, head), head)

    def attend(h, carry):
        scores = tn(qkv_t[head_rows(h, 1), :], qkv_t[head_rows(h, 0), :]) + key_bias
        top = jnp.max(scores, 0, keepdims=True)
        weights = jnp.exp(scores - top)
        inverse = 1.0 / jnp.sum(weights, 0, keepdims=True)
        weights_low = weights.astype(BF)
        expo[aligned(h, seq_len), :] = weights_low
        inv_sum[aligned(h, 8), :] = jnp.broadcast_to(inverse, (8, seq_len))
        att_t[head_rows(h, 0), :] = (nn(qkv_t[head_rows(h, 2), :], weights_low) * inverse).astype(BF)
        return carry

    lax.fori_loop(0, H, attend, 0, unroll=6)

    loads[1].wait()
    summed = x_t[...].astype(F32) + (tn(w_o[...], att_t[...]) + column(V_BO))
    centred = summed - jnp.mean(summed, 0, keepdims=True)
    inv_one = lax.rsqrt(jnp.mean(centred * centred, 0, keepdims=True) + 1e-12)
    normed_one[...] = centred * inv_one
    middle_low[...] = (normed_one[...] * column(V_G1) + column(V_S1)).astype(BF)

    loads[2].wait()
    for i in range(parts):
        rows = slice(i * width, (i + 1) * width)
        pre = tn(w_in[:, rows], middle_low[...]) + column(V_BIN + i)
        cumulative = 0.5 * (1.0 + lax.erf(pre * 0.7071067811865476))
        density = jnp.exp(-0.5 * pre * pre) * 0.3989422804014327
        act[rows, :] = (pre * cumulative).astype(BF)
        slope[rows, :] = (cumulative + pre * density).astype(BF)
    loads[3].wait()
    middle = normed_one[...] * column(V_G1) + column(V_S1)
    summed = middle + (tn(w_out[...], act[...]) + column(V_BOUT))
    centred = summed - jnp.mean(summed, 0, keepdims=True)
    inv_two = lax.rsqrt(jnp.mean(centred * centred, 0, keepdims=True) + 1e-12)
    normed_two[...] = centred * inv_two
    finish(cot_copies)
    grad_final = jnp.transpose(cot_rows[...].reshape(seq_len, width)).astype(F32)
    grad_final = grad_final + column(V_CP) * (live * inv_len)
    low_a[...] = norm_back(grad_final * column(V_G2), normed_two[...], inv_two).astype(BF)

    def whole_grad(m):
        if m == G_OUT:
            rows, columns = act, low_a
        elif m == G_IN:
            rows, columns = middle_low, slope
        elif m == G_O:
            rows, columns = att_t, low_a
        else:
            rows, columns = x_t, qkv_t
        return rows, columns

    def put(m):
        rows, columns = whole_grad(m)
        for i in range(rows.shape[0] // width):
            value = nt(rows[i * width : (i + 1) * width, :], columns[...])
            here = stage.at[:, 0 : value.shape[1]]
            here[...] = value.astype(BF)
            copy = pltpu.make_async_copy(
                here, grad_refs[m].at[i * width : (i + 1) * width, :], put_sem.at[0]
            )
            copy.start()
            copy.wait()

    flight = {}

    def partial(m, which):
        rows, columns = whole_grad(m)
        deep = rows.shape[0] // batch_count
        left = jnp.concatenate([rows[aligned(2 * j + which, deep), :] for j in range(4)], 0)
        tile = width // 2
        half = columns.shape[0] // 2
        for h in range(2):
            value = nt(left, columns[h * half : (h + 1) * half, :])
            for j in range(4):
                for t in range(half // tile):
                    block = value[j * deep : (j + 1) * deep, t * tile : (t + 1) * tile]
                    yield h, j, slice(t * deep, (t + 1) * deep), block

    def core_buffer(m):
        rows = held_core[m].shape[3]
        start = held_core[G_O].shape[3] if m == G_QKV else 0
        return send_core.at[:, :, :, start : start + rows, :]

    def core_start(m):
        buffer = core_buffer(m)
        if m == G_IN:
            for copy in flight[G_OUT, 0]:
                copy.wait_send()
        if m == G_O:
            for copy in flight[G_IN, 0]:
                copy.wait_send()
        for h, j, rows, block in partial(m, 1 - core):
            buffer[h, j // 2, j % 2, rows, :] = block.astype(BF)
        flight[m, 0] = [
            remote(buffer, held_core[m], to_core, core_send.at[m, 0], core_recv.at[m, 0])
        ]

    def core_add(m):
        for copy in flight[m, 0]:
            copy.wait_recv()
            if m in (G_O, G_QKV):
                copy.wait_send()
        held = held_core[m]
        for h, j, rows, block in partial(m, core):
            held[h, j // 2, j % 2, rows, :] = add_low(held[h, j // 2, j % 2, rows, :], block)

    def first_link(m):
        held = held_core[m]
        flight[m, 1] = [
            remote(
                held.at[0, :, 1 - at_x],
                held_one[m].at[0],
                to_x,
                link_send.at[m, 0],
                link_recv.at[m, 0],
            ),
            remote(
                held.at[1, 1 - at_y],
                held_one[m].at[1],
                to_y,
                link_send.at[m, 1],
                link_recv.at[m, 1],
            ),
        ]

    order = ((1 - at_y, 1 - at_x), (at_y, 1 - at_x), (1 - at_y, at_x), (at_y, at_x))

    def first_block(y, x, which):
        deep = ff // batch_count
        row = aligned(4 * y + 2 * x + which, deep)
        return nt(act[row, :], low_a[...])

    def first_send(k):
        y, x = order[k]
        value = first_block(y, x, 1 - core)
        half = value.shape[1] // 2
        send_core[0, y, x] = value[:, :half].astype(BF)
        send_core[1, y, x] = value[:, half:].astype(BF)
        flight[G_OUT, 0].append(
            remote(
                send_core.at[:, y, x],
                held_core[G_OUT].at[:, y, x],
                to_core,
                core_send.at[G_OUT, k],
                core_recv.at[G_OUT, k],
            )
        )

    def first_add(k):
        held, after = held_core[G_OUT], held_one[G_OUT]
        y, x = order[k]
        value = first_block(y, x, core)
        half = value.shape[1] // 2
        flight[G_OUT, 0][k].wait_recv()
        held[0, y, x] = add_low(held[0, y, x], value[:, :half])
        held[1, y, x] = add_low(held[1, y, x], value[:, half:])
        hops = []
        if k in (0, 1):
            hops.append((0, after.at[0, y], to_x, k))
        if k in (0, 2):
            hops.append((1, after.at[1, x], to_y, 2 + k // 2))
        for h, dst, device, sem in hops:
            flight[G_OUT, 1].append(
                remote(
                    held.at[h, y, x],
                    dst,
                    device,
                    link_send.at[G_OUT, sem],
                    link_recv.at[G_OUT, sem],
                )
            )

    def first_sums():
        flight[G_OUT, 0], flight[G_OUT, 1] = [], []
        first_send(0)
        first_send(1)
        first_add(0)
        first_send(2)
        first_send(3)
        for k in range(1, 4):
            first_add(k)

    def second_link(m):
        finish(flight[m, 1])
        held, after = held_core[m], held_one[m]
        after[0, 1 - at_y] = add_low(after[0, 1 - at_y], held[0, 1 - at_y, at_x])
        after[1, 1 - at_x] = add_low(after[1, 1 - at_x], held[1, at_y, 1 - at_x])
        flight[m, 2] = [
            remote(
                after.at[0, 1 - at_y],
                held_two[m].at[0],
                to_y,
                link_send.at[m, 4],
                link_recv.at[m, 4],
            ),
            remote(
                after.at[1, 1 - at_x],
                held_two[m].at[1],
                to_x,
                link_send.at[m, 5],
                link_recv.at[m, 5],
            ),
        ]
        after[0, at_y] = add_low(after[0, at_y], held[0, at_y, at_x])
        after[1, at_x] = add_low(after[1, at_x], held[1, at_y, at_x])

    def first_z(m):
        finish(flight[m, 2])
        after, last, ready = held_one[m], held_two[m], held_z[m]
        for h in range(2):
            mine = after[0, at_y] if h == 0 else after[1, at_x]
            block = last[h].astype(F32) + mine.astype(F32)
            if m == G_IN:
                deep = block.shape[0] // 2
                for k in range(2):
                    ready[h, k] = block[k * deep : (k + 1) * deep, :].astype(BF)
                continue
            deep = grad_refs[m].shape[0]
            per_row = width // 256
            count = block.shape[0] // deep * per_row
            tiles = []
            for t in range(count):
                row, lane = t // per_row * deep, t % per_row * 128
                tiles.append(block[row : row + deep, lane : lane + 128])
            full = count // 2
            for k in range(2):
                for t in range(full):
                    ready[h, k, t * deep : (t + 1) * deep, :] = tiles[t + k * (full + 1)].astype(BF)
            turned = pltpu.roll(tiles[full], 64, 1)
            left = lax.broadcasted_iota(jnp.int32, (deep // 2, 128), 1) < 64
            upper, lower = slice(0, deep // 2), slice(deep // 2, deep)
            folded = (
                jnp.where(left, tiles[full][upper], turned[lower]),
                jnp.where(left, turned[upper], tiles[full][lower]),
            )
            for k in range(2):
                ready[h, k, full * deep :, :] = folded[k].astype(BF)
        flight[m, 3] = [
            remote(
                ready.at[:, 1 - z_lo], z_one[m], to_z_lo, link_send.at[m, 6], link_recv.at[m, 6]
            )
        ]

    def second_z(m):
        finish(flight[m, 3])
        z_one[m][1 - z_hi] = add_low(z_one[m][1 - z_hi], held_z[m][1 - z_hi, z_lo])
        flight[m, 4] = [
            remote(
                z_one[m].at[1 - z_hi], z_two[m], to_z_hi, link_send.at[m, 7], link_recv.at[m, 7]
            )
        ]

    def last_sum(m):
        mine = z_one[m][z_hi].astype(F32) + held_z[m][z_hi, z_lo].astype(F32)
        finish(flight[m, 4])
        total = mine + z_two[m][...].astype(F32)
        out = grad_refs[m]
        deep, wide = out.shape
        if m == G_IN:
            out[:, : wide // 2] = total[:deep, :]
            out[:, wide // 2 :] = total[deep:, :]
            return
        full = wide // 128
        tiles = [total[t * deep : (t + 1) * deep, :] for t in range(full)]
        folded = total[full * deep :, :]
        turned = pltpu.roll(folded, 64, 1)
        after_tiles = jnp.concatenate(tiles + [jnp.concatenate([folded, turned], 0)], 1)
        before_tiles = jnp.concatenate([jnp.concatenate([turned, folded], 0)] + tiles, 1)
        before_tiles = pltpu.roll(before_tiles, full * 128 + 64, 1)
        out[...] = jnp.where(z_lo == 0, after_tiles, before_tiles)[:, :wide]

    peers = (to_core, to_x, to_y, to_z_lo, to_z_hi)

    def vector_start():
        vec_own[0] = jnp.transpose(vec_cols[...])[0:16, :]
        flight["v"] = remote(vec_own.at[0], vec_in.at[0], peers[0], v_send.at[0], v_recv.at[0])

    def vector_step(k):
        flight["v"].wait()
        total = vec_own[k] + vec_in[k]
        if k == 4:
            vecs_ref[...] = total
        else:
            vec_own[k + 1] = total
            flight["v"] = remote(
                vec_own.at[k + 1],
                vec_in.at[k + 1],
                peers[k + 1],
                v_send.at[k + 1],
                v_recv.at[k + 1],
            )

    if fused:
        first_sums()
    else:
        put(G_OUT)

    rows_out = x_rows
    output = normed_two[...] * column(V_G2) + column(V_S2)
    rows_out[...] = jnp.transpose(output.astype(BF)).reshape(seq_count, block_len, width)
    out_copies = exchange(rows_out, out_ref, 2, o_send, o_recv)
    pooled_col = jnp.sum(output * (live * inv_len), 1, keepdims=True)
    if fused:
        pool_own[...] = jnp.transpose(jnp.broadcast_to(pooled_col, (width, 128)))[0:8, :]
        pool_in[me_s] = pool_own[...]
        flight["p"] = [
            remote(pool_own, pool_in.at[me_s], seq_peer(d), p_send.at[d], p_recv.at[d])
            for d in range(1, seq_count)
        ]
    else:
        vec_cols[:, 12:13] = pooled_col
    grad_final = jnp.transpose(cot_rows[...].reshape(seq_len, width)).astype(F32)
    grad_final = grad_final + column(V_CP) * (live * inv_len)
    vec_cols[:, 0:1] = jnp.sum(grad_final * normed_two[...], 1, keepdims=True)
    vec_cols[:, 1:2] = jnp.sum(grad_final, 1, keepdims=True)
    vec_cols[:, 2:3] = jnp.sum(low_a[...].astype(F32), 1, keepdims=True)

    for i in range(parts):
        rows = slice(i * width, (i + 1) * width)
        grad_act_low = nn(w_out[rows, :], low_a[...]).astype(BF)
        grad_pre = (grad_act_low.astype(F32) * slope[rows, :].astype(F32)).astype(BF)
        slope[rows, :] = grad_pre
        vec_cols[:, 3 + i : 4 + i] = jnp.sum(grad_pre.astype(F32), 1, keepdims=True)
    if fused:
        core_start(G_IN)
    else:
        put(G_IN)
    grad_middle = low_a[...].astype(F32) + nn(w_in[...], slope[...])
    if fused:
        second_link(G_OUT)

    vec_cols[:, 7:8] = jnp.sum(grad_middle * normed_one[...], 1, keepdims=True)
    vec_cols[:, 8:9] = jnp.sum(grad_middle, 1, keepdims=True)
    grad_first = normed_two
    grad_first[...] = norm_back(grad_middle * column(V_G1), normed_one[...], inv_one)
    low_a[...] = grad_first[...].astype(BF)
    vec_cols[:, 9:10] = jnp.sum(low_a[...].astype(F32), 1, keepdims=True)
    if fused:
        core_add(G_IN)
        first_link(G_IN)
        core_start(G_O)
    else:
        put(G_O)
    grad_heads = nn(w_o[...], low_a[...])
    for h in range(H):
        rows = slice(h * head, (h + 1) * head)
        grad_att[rows, :] = (grad_heads[rows, :] * inv_sum[h * 8 : h * 8 + 1, :]).astype(BF)
    if fused:
        core_add(G_O)

    def attend_back(h, carry):
        grad = grad_att[head_rows(h, 0), :]
        inner = jnp.sum(grad.astype(F32) * att_t[head_rows(h, 0), :].astype(F32), 0, keepdims=True)
        weights_low = expo[aligned(h, seq_len), :]
        queries, keys, values = (qkv_t[head_rows(h, third), :] for third in range(3))
        grad_probs = tn(values, grad)
        grad_scores = (weights_low.astype(F32) * (grad_probs - inner)).astype(BF)
        qkv_t[head_rows(h, 0), :] = (nn(keys, grad_scores) * scale).astype(BF)
        qkv_t[head_rows(h, 1), :] = nt(queries, grad_scores).astype(BF)
        qkv_t[head_rows(h, 2), :] = nt(grad, weights_low).astype(BF)
        return carry

    if fused:
        for k in range(3):
            lax.fori_loop(k * (H // 3), (k + 1) * (H // 3), attend_back, 0)
            if k == 0:
                first_z(G_OUT)
    else:
        lax.fori_loop(0, H, attend_back, 0)
    vec_cols[:, 10:11] = jnp.sum(qkv_t[0:width, :].astype(F32), 1, keepdims=True)
    vec_cols[:, 11:12] = jnp.sum(qkv_t[2 * width :, :].astype(F32), 1, keepdims=True)
    if fused:
        vector_start()
        core_start(G_QKV)
    grad_in = nn(w_qkv[...], qkv_t[...]) + grad_first[...]
    rows_gin = cot_rows
    rows_gin[...] = jnp.transpose(grad_in.astype(BF)).reshape(seq_count, block_len, width)
    if fused:
        second_z(G_OUT)
    gin_copies = exchange(rows_gin, gin_ref, 3, g_send, g_recv)
    if fused:
        second_link(G_IN)
        core_add(G_QKV)
        vector_step(0)
        first_link(G_O)
        first_z(G_IN)
        first_link(G_QKV)
        last_sum(G_OUT)
        vector_step(1)
        second_z(G_IN)
        second_link(G_QKV)
        second_link(G_O)
        vector_step(2)
        first_z(G_QKV)
        first_z(G_O)
        last_sum(G_IN)
        vector_step(3)
        second_z(G_QKV)
        second_z(G_O)
        finish(flight["p"])
        for k in range(seq_count):
            pooled_ref[k : k + 1, :] = pool_in[k, 0:1, :]
        vector_step(4)
        last_sum(G_QKV)
        last_sum(G_O)
    else:
        put(G_QKV)
        vecs_ref[...] = jnp.transpose(vec_cols[...])[0:16, :]
        pooled_ref[...] = jnp.transpose(vec_cols[...])[12:16, :]
    finish(out_copies)
    finish(gin_copies)


def deliver_kernel(*refs):
    out_in, gin_in, pooled_in, vecs_in = refs[:4]
    grads_in = refs[4:8]
    out_ref, gin_ref, pooled_ref = refs[8:11]
    grad_refs, vec_refs = refs[11:15], refs[15:24]
    grad_refs[0][...] = jnp.transpose(grads_in[0][...])
    moves = [(out_in, out_ref), (gin_in, gin_ref), (pooled_in, pooled_ref)]
    for src, dst in moves + list(zip(grads_in[1:], grad_refs[1:])):
        dst[...] = src[...]
    width = vecs_in.shape[1]
    for row, ref in zip((10, 11, 9, 7, 8, 3, 2, 0, 1), vec_refs):
        for i in range(ref.shape[0] // width):
            ref[i * width : (i + 1) * width] = vecs_in[row + i : row + i + 1, :].reshape(width)


def deliver(outs):
    out_hidden, grad_in, pooled, total, g_out, g_in, g_o, g_qkv = outs
    ff = total.shape[1] * g_out.shape[0] // g_qkv.shape[0]
    vmem = pl.BlockSpec(memory_space=pltpu.VMEM)
    arrays = (out_hidden, grad_in, pooled, g_out, g_in, g_o, g_qkv)
    lengths = [total.shape[1]] * 5 + [ff] + [total.shape[1]] * 3
    vectors = tuple(jax.ShapeDtypeStruct((n,), F32) for n in lengths)
    shapes = [jax.ShapeDtypeStruct(a.shape, a.dtype) for a in arrays]
    shapes[3] = jax.ShapeDtypeStruct(g_out.shape[::-1], F32)
    results = pl.pallas_call(
        deliver_kernel,
        out_shape=tuple(shapes) + vectors,
        in_specs=[vmem] * 8,
        out_specs=(vmem,) * 16,
        name="deliver",
    )(*outs)
    out_hidden, grad_in, pooled, g_out, g_in, g_o, g_qkv = results[:7]
    b_q, b_v, b_o, gain_one, shift_one, b_in, b_out, gain_two, shift_two = results[7:]
    return (
        out_hidden,
        pooled,
        grad_in,
        g_qkv,
        b_q,
        b_v,
        g_o,
        b_o,
        gain_one,
        shift_one,
        g_in,
        b_in,
        g_out.T,
        b_out,
        gain_two,
        shift_two,
    )


def body(
    hidden_in,
    lengths,
    w_qkv,
    b_q,
    b_v,
    w_o,
    b_o,
    gain_one,
    shift_one,
    w_in,
    b_in,
    w_out,
    b_out,
    gain_two,
    shift_two,
    cot_hidden,
    cot_pooled,
):
    batch_count, seq_count = lax.axis_size("batch"), lax.axis_size("seq")
    seqs_here, block_len, width = hidden_in.shape
    ff = w_in.shape[1]
    seq_len = seq_count * block_len
    assert seqs_here == seq_count
    fused = batch_count == 8 and seq_count == 4

    anywhere = pl.BlockSpec(memory_space=pl.ANY)
    vmem = pl.BlockSpec(memory_space=pltpu.VMEM)
    smem = pl.BlockSpec(memory_space=pltpu.SMEM)
    rows = jax.ShapeDtypeStruct(hidden_in.shape, BF)
    weights = (w_out, w_in, w_o, w_qkv)
    if fused:
        grads = tuple(
            jax.ShapeDtypeStruct((w.shape[0] // batch_count, w.shape[1] // seq_count), F32)
            for w in weights
        )
    else:
        grads = tuple(jax.ShapeDtypeStruct(w.shape, BF) for w in weights)
    dma = pltpu.SemaphoreType.DMA
    scratch = [pltpu.VMEM(w.shape, BF) for w in (w_qkv, w_o, w_in, w_out)]
    scratch += [
        pltpu.VMEM((seq_count, block_len, width), BF),
        pltpu.VMEM((seq_count, block_len, width), BF),
        pltpu.VMEM((width, seq_len), BF),
        pltpu.VMEM((3 * width, seq_len), BF),
        pltpu.VMEM((H * seq_len, seq_len), BF),
        pltpu.VMEM((H * 8, seq_len), F32),
        pltpu.VMEM((width, seq_len), BF),
        pltpu.VMEM((width, seq_len), F32),
        pltpu.VMEM((width, seq_len), BF),
        pltpu.VMEM((ff, seq_len), BF),
        pltpu.VMEM((ff, seq_len), BF),
        pltpu.VMEM((width, seq_len), F32),
        pltpu.VMEM((width, seq_len), BF),
        pltpu.VMEM((width, seq_len), BF),
        pltpu.VMEM((width, 128), F32),
        dma((4,)),
        dma((4,)),
    ]
    scratch += [dma((seq_count,))] * 8
    if fused:
        deep = width // batch_count
        blocks = (
            (ff // batch_count, width // 2),
            (deep * (ff // width), width // 2),
            (deep, width // 2),
            (deep * 3, width // 2),
        )
        z_blocks = tuple(
            (block[0] // 2, block[1]) if m == G_IN else (block[0] * block[1] // 256, 128)
            for m, block in enumerate(blocks)
        )
        scratch += [pltpu.VMEM((2, 2, 2) + blocks[0], BF)]
        scratch += [pltpu.VMEM((2, 2, 2) + block, BF) for block in blocks]
        scratch += [pltpu.VMEM((2, 2) + block, BF) for block in blocks]
        scratch += [pltpu.VMEM((2,) + block, BF) for block in blocks]
        scratch += [pltpu.VMEM((2, 2) + block, BF) for block in z_blocks]
        scratch += [pltpu.VMEM((2,) + block, BF) for block in z_blocks]
        scratch += [pltpu.VMEM(block, BF) for block in z_blocks]
        scratch += [dma((4, 4)), dma((4, 4)), dma((4, 8)), dma((4, 8))]
        scratch += [
            pltpu.VMEM((5, 16, width), F32),
            pltpu.VMEM((5, 16, width), F32),
            pltpu.VMEM((8, width), F32),
            pltpu.VMEM((seq_count, 8, width), F32),
            dma((5,)),
            dma((5,)),
            dma((seq_count,)),
            dma((seq_count,)),
        ]
    else:
        scratch += [pltpu.VMEM((width, ff), BF), dma((1,))]
    outs = pl.pallas_call(
        functools.partial(
            layer_kernel, (batch_count, seq_count, block_len, width, ff, fused)
        ),
        out_shape=(
            rows,
            rows,
            jax.ShapeDtypeStruct((seq_count, width), F32),
            jax.ShapeDtypeStruct((16, width), F32),
        )
        + grads,
        in_specs=[anywhere, anywhere, smem] + [vmem] * 10 + [anywhere] * 4,
        out_specs=(anywhere, anywhere, vmem, vmem) + (vmem if fused else anywhere,) * 4,
        scratch_shapes=scratch,
        compiler_params=pltpu.CompilerParams(
            collective_id=0, has_side_effects=True, vmem_limit_bytes=63 * 2**20
        ),
        name="encoder_layer",
    )(
        hidden_in,
        cot_hidden,
        lengths,
        cot_pooled,
        b_q,
        b_v,
        b_o,
        gain_one,
        shift_one,
        b_out,
        gain_two,
        shift_two,
        b_in,
        w_qkv,
        w_o,
        w_in,
        w_out,
    )
    if fused:
        return deliver(outs)
    out_hidden, grad_in, pooled, total, g_out, g_in, g_o, g_qkv = outs
    pooled = lax.all_gather(pooled[0], "seq", axis=0)
    total = lax.psum(total[:12], ("batch", "seq"))

    def scatter(grad):
        part = lax.psum_scatter(grad.astype(F32), "batch", scatter_dimension=0, tiled=True)
        part = lax.psum_scatter(part.astype(BF), "seq", scatter_dimension=1, tiled=True)
        return part.astype(F32)

    g_out, g_in, g_o, g_qkv = (scatter(g) for g in (g_out, g_in, g_o, g_qkv))
    return (
        out_hidden,
        pooled,
        grad_in,
        g_qkv,
        total[10],
        total[11],
        g_o,
        total[9],
        total[7],
        total[8],
        g_in,
        total[3:7].reshape(ff),
        g_out,
        total[2],
        total[0],
        total[1],
    )


def solution(mesh):
    rows = P("batch", "seq", None)
    shard = P("batch", "seq")
    in_specs = (rows, P("batch")) + (P(),) * 13 + (rows, P("batch", None))
    out_specs = (
        rows,
        P("batch", None),
        rows,
        shard,
        P(),
        P(),
        shard,
        P(),
        P(),
        P(),
        shard,
        P(),
        shard,
        P(),
        P(),
        P(),
    )
    return jax.shard_map(body, mesh=mesh, in_specs=in_specs, out_specs=out_specs, check_vma=False)
```
